512 devices in a mesh: seq: 64 (over y, z), chan: 8 (over x, core).
Axes of the slice: x: 4, y: 8, z: 8, core: 2. Of those that a mesh axis runs over, the one named last changes fastest.
Arguments:
- signal: bfloat16 [8192, 4096], P('seq', 'chan'), may hold values from -6 to 6
- gates: bfloat16 [8192, 4096], P('seq', 'chan'), may hold values from -6 to 6
- filters: bfloat16 [8192, 4096], P('seq', 'chan'), may hold values from -1 to 1
- skip_gain: float32 [4096], P('chan'), may hold values from 0.5 to 1.5
- out_proj: bfloat16 [4096, 4096], P('chan', 'seq'), may hold values from -0.09375 to 0.09375
- cotangent: bfloat16 [8192, 4096], P('seq', 'chan'), may hold values from -6 to 6
Outputs:
- mixed: bfloat16 [8192, 4096], P('seq', 'chan')
- grad_signal: bfloat16 [8192, 4096], P('seq', 'chan')
- grad_gates: bfloat16 [8192, 4096], P('seq', 'chan')
- grad_filters: bfloat16 [8192, 4096], P('seq', 'chan')
The draws below stay inside these ranges and needn't reach their ends.
All inputs are finite; a program needn't handle non-finite values.
Results may differ from the reference program's by a relative error of at most 0.01.
Values may be sent and summed in bfloat16 or wider, within the bound.
A program may use at most 64 MiB of HBM per device.

```python
import math
import jax
import jax.numpy as jnp
from jax import lax

CHANNELS = 4096
TEXT_LENGTH = 8192


def draw_filters(key, part):
    key = jax.random.fold_in(key, 11)
    generator_starting_states = jax.random.split(key, 6)
    loop_round_amount = jnp.arange(TEXT_LENGTH, dtype=jnp.float32)[:, None]
    slow_share = 0.5
    stochastic_jitter = jnp.clip(jax.random.normal(generator_starting_states[0], (TEXT_LENGTH, CHANNELS), jnp.float32), -3.5, 3.5)
    slow_mask = jax.random.bernoulli(generator_starting_states[1], slow_share, (CHANNELS,))
    fast_rate = jnp.exp(jax.random.uniform(generator_starting_states[2], (CHANNELS,), jnp.float32, math.log(1.0 / 50.0), math.log(1.0 / 30.0)))
    slow_rate = jnp.exp(jax.random.uniform(generator_starting_states[3], (CHANNELS,), jnp.float32, math.log(0.1), math.log(2.0))) / TEXT_LENGTH
    happening_frequency = jnp.where(slow_mask, slow_rate, fast_rate)
    jitter_magnitude = jnp.sqrt(-jnp.expm1(-2.0 * happening_frequency))
    impulse_offset = jax.random.randint(generator_starting_states[4], (3,), 0, TEXT_LENGTH).astype(jnp.float32)
    impulse_kept_indicators = jax.random.uniform(generator_starting_states[5], (3,), jnp.float32, 0.5, 0.8)
    impulse_occurrences = jnp.prod(jnp.where(loop_round_amount[:, :, None] >= impulse_offset, impulse_kept_indicators, 1.0), axis=-1)
    drawn_numbers = stochastic_jitter * jnp.exp(-happening_frequency[None, :] * loop_round_amount) * jitter_magnitude[None, :] * impulse_occurrences
    return drawn_numbers.astype(jnp.bfloat16)


def level_of(rng, extent, shards, smallest, largest):
    def one(dim, parts):
        steps = jax.random.uniform(jax.random.fold_in(jax.random.fold_in(rng, 6), dim), (parts,), jnp.float32, smallest / len(shards), largest / len(shards))
        return jnp.repeat(jnp.exp(steps), extent[dim] // parts).reshape((-1,) + (1,) * (len(extent) - dim - 1))

    level = one(*shards[0])
    for cut in shards[1:]:
        level = level * one(*cut)
    return level


def bell_draw(stream_key, shape, width, limit, cuts=(), kind=jnp.bfloat16):
    entries = width * jax.random.normal(stream_key, shape, jnp.float32)
    if cuts:
        entries = entries * level_of(stream_key, shape, cuts, -0.22, 0.18)
    return jnp.clip(entries, -limit, limit).astype(kind)


def setup_inputs(seed: int = 0) -> dict:
    seeds = jax.random.split(jax.random.key(seed), 7)
    signal = bell_draw(seeds[0], (TEXT_LENGTH, CHANNELS), 1.0, 6.0, ((0, 64), (1, 8)))
    gates = bell_draw(seeds[1], (TEXT_LENGTH, CHANNELS), 1.0, 6.0, ((0, 64), (1, 8)))
    filters = draw_filters(jax.random.fold_in(seeds[6], 71), 0)
    skip_gain = jnp.clip(0.5 + 1.0 * jax.random.uniform(seeds[3], (CHANNELS,), jnp.float32) ** level_of(seeds[3], (CHANNELS,), ((0, 8),), -0.2, 0.2), 0.5, 1.5)
    out_proj = bell_draw(seeds[4], (CHANNELS, CHANNELS), CHANNELS ** -0.5, 0.09375, ((0, 8), (1, 64)))
    cotangent = bell_draw(seeds[5], (TEXT_LENGTH, CHANNELS), 1.0, 6.0, ((0, 64), (1, 8)))
    return {"signal": signal, "gates": gates, "filters": filters, "skip_gain": skip_gain, "out_proj": out_proj, "cotangent": cotangent}


def spectrum(drawn_numbers):
    return jnp.fft.rfft(drawn_numbers, n=2 * TEXT_LENGTH, axis=0)

def convolve(first_arr, second_arr):
    return jnp.fft.irfft(spectrum(first_arr) * spectrum(second_arr), n=2 * TEXT_LENGTH, axis=0)[:TEXT_LENGTH]

def correlate(grad_arr, kernel_arr):
    return jnp.fft.irfft(jnp.conj(spectrum(kernel_arr)) * spectrum(grad_arr), n=2 * TEXT_LENGTH, axis=0)[:TEXT_LENGTH]

def by_blocks(function, *arrays):
    block = min(512, CHANNELS)
    block_count = CHANNELS // block
    stacked = tuple((a.reshape(TEXT_LENGTH, block_count, block).transpose(1, 0, 2) for a in arrays))
    mapped = lax.map(lambda members: function(*members), stacked)
    return mapped.transpose(1, 0, 2).reshape(TEXT_LENGTH, CHANNELS)

def reference(signal, gates, filters, skip_gain, out_proj, cotangent):
    signal_f = signal.astype(jnp.float32)
    gates_f = gates.astype(jnp.float32)
    filters_f = filters.astype(jnp.float32)
    convolved = by_blocks(convolve, signal_f, filters_f)
    before_gate = convolved + skip_gain[None, :] * signal_f
    gated = (before_gate * gates_f).astype(jnp.bfloat16)
    mixed = jnp.dot(gated, out_proj, preferred_element_type=jnp.float32).astype(jnp.bfloat16)
    grad_gated = jnp.dot(cotangent, out_proj.T, preferred_element_type=jnp.float32)
    grad_gates = (grad_gated * before_gate).astype(jnp.bfloat16)
    grad_conv = (grad_gated * gates_f).astype(jnp.bfloat16)
    grad_conv_f = grad_conv.astype(jnp.float32)
    grad_through = by_blocks(correlate, grad_conv_f, filters_f)
    grad_signal = (grad_through + skip_gain[None, :] * grad_conv_f).astype(jnp.bfloat16)
    grad_kernel = by_blocks(correlate, grad_conv_f, signal_f)
    grad_filters = (grad_kernel * (1.0 / math.sqrt(TEXT_LENGTH))).astype(jnp.bfloat16)
    return (mixed, grad_signal, grad_gates, grad_filters)
```

```python
import functools
import math

import jax
import jax.numpy as jnp
import ml_dtypes
import numpy as np
from jax import lax
from jax.experimental import pallas as pl
from jax.experimental.pallas import tpu as pltpu
from jax.sharding import PartitionSpec as P

LANES = 128
GROUP = 8
CORES = 2
MESH = pl.DeviceIdType.MESH
F32 = jnp.float32
BF16 = jnp.bfloat16


def halves(table):
    high = table.astype(ml_dtypes.bfloat16)
    low = (table - high.astype(np.float64)).astype(ml_dtypes.bfloat16)
    return high, low


def make_tables(blocks):
    total = 2 * blocks * LANES
    rows = -(-(blocks + 1) // 8) * 8
    k = np.arange(rows)
    j = np.arange(blocks)
    b = np.arange(LANES)
    live = (k <= blocks)[:, None].astype(np.float64)
    outer = 2 * np.pi * ((k[:, None] * j[None, :]) % (2 * blocks)) / (2 * blocks)
    first = np.concatenate([live * np.cos(outer), -live * np.sin(outer)], axis=0)
    twist = 2 * np.pi * k[:, None] * b[None, :] / total
    inner = 2 * np.pi * ((b[:, None] * b[None, :]) % LANES) / LANES
    cos, sin = np.cos(inner), np.sin(inner)
    second = np.block([[cos, -sin], [sin, cos]])
    weight = np.where((k == 0) | (k == blocks), 1.0, 2.0)[:, None] * live / total
    last = np.concatenate([weight * np.cos(outer), -weight * np.sin(outer)], axis=0).T
    return (
        np.concatenate(halves(first), axis=1),
        np.stack([np.cos(twist), -np.sin(twist)]).astype(np.float32),
        np.stack(halves(second)),
        np.stack(halves(second.T)),
        np.stack(halves(last)),
    )


def split(value):
    high = value.astype(BF16)
    return high, (value - high.astype(F32)).astype(BF16)


def mm(left, right):
    return jnp.dot(left, right, preferred_element_type=F32)


def forward(x, first, twist, second):
    rows = twist.shape[1]
    mid = mm(first[...], jnp.concatenate([x, x], axis=0))
    cos, sin = twist[0], twist[1]
    pieces = []
    for c in range(GROUP):
        re = mid[:rows, c * LANES : (c + 1) * LANES]
        im = mid[rows:, c * LANES : (c + 1) * LANES]
        pieces.append(jnp.concatenate([re * cos - im * sin, re * sin + im * cos], axis=1))
    high, low = split(jnp.concatenate(pieces, axis=0))
    return mm(high, second[0]) + mm(low, second[0]) + mm(high, second[1])


def inverse(spec, twist, back, last):
    rows = twist.shape[1]
    high, low = split(spec)
    mid = mm(high, back[0]) + mm(low, back[0]) + mm(high, back[1])
    cos, sin = twist[0], twist[1]
    pieces = []
    for c in range(GROUP):
        re = mid[c * rows : (c + 1) * rows, :LANES]
        im = mid[c * rows : (c + 1) * rows, LANES:]
        pieces.append(jnp.concatenate([re * cos + im * sin, im * cos - re * sin], axis=0))
    high, low = split(jnp.concatenate(pieces, axis=1))
    return mm(last[0], high) + mm(last[1], high) + mm(last[0], low)


def times(a, b):
    ar, ai, br, bi = a[:, :LANES], a[:, LANES:], b[:, :LANES], b[:, LANES:]
    return jnp.concatenate([ar * br - ai * bi, ar * bi + ai * br], axis=1)


def times_conj(a, b):
    ar, ai, br, bi = a[:, :LANES], a[:, LANES:], b[:, :LANES], b[:, LANES:]
    return jnp.concatenate([ar * br + ai * bi, ar * bi - ai * br], axis=1)


def kernel(
    ny,
    nz,
    nx,
    sig,
    gat,
    fil,
    skip,
    wgt,
    cot,
    first,
    twist,
    second,
    back,
    last,
    mixed,
    grad_sig,
    grad_gat,
    grad_fil,
    out16,
    in16,
    out8,
    in8,
    gout8,
    gin8,
    rout16,
    rin16,
    rows32,
    sf_spec,
    wt,
    call,
    grad,
    own,
    ex_out,
    ex_in,
    mx_out,
    mx_in,
    a2a_send,
    a2a_recv,
    w_send,
    w_first,
    w_ring,
    c_send,
    c_recv,
    m_send,
    m_recv,
):
    nseq = ny * nz
    chans = GROUP * nseq
    s = lax.axis_index("seq")
    c = lax.axis_index("chan")
    y, z = s // nz, s % nz
    x, core = c // CORES, c % CORES
    sibling = x * CORES + (1 - core)
    block = wgt.shape[1]
    half = block // 2

    def x_peer(dx):
        return ((x + dx) % nx) * CORES + core

    bar = pltpu.get_barrier_semaphore()

    def greet(i, carry):
        pl.semaphore_signal(bar, inc=1, device_id={"seq": (s + i) % nseq}, device_id_type=MESH)
        return carry

    lax.fori_loop(1, nseq, greet, 0)
    for dx in range(1, nx):
        pl.semaphore_signal(bar, inc=1, device_id={"chan": x_peer(dx)}, device_id_type=MESH)
    pl.semaphore_signal(bar, inc=1, device_id={"chan": sibling}, device_id_type=MESH)
    pl.semaphore_wait(bar, nseq + nx - 1)

    def send(src, dst, send_sem, recv_sem, **where):
        pltpu.make_async_remote_copy(
            src_ref=src,
            dst_ref=dst,
            send_sem=send_sem,
            recv_sem=recv_sem,
            device_id=where,
            device_id_type=MESH,
        ).start()

    def wait(ref, sem):
        pltpu.make_async_copy(ref, ref, sem).wait()

    def w_rows(h, yy, zz):
        start = pl.multiple_of((yy * nz + zz) * block + h * half, half)
        return wt.at[pl.ds(start, half)]

    def ring_seq(h, step):
        if h == 0:
            return y * nz + (z + step) % nz
        return ((y + step) % ny) * nz + z

    def ring_block(h, offset, i):
        if h == 0:
            return w_rows(0, (y - i) % ny, (z + offset) % nz)
        return w_rows(1, (y + offset) % ny, (z - i) % nz)

    size = ny
    reach = size // 2

    def pass_on(h, way, d, i):
        sign = 1 if way == 0 else -1
        ref = ring_block(h, -sign * (d - 1), i)
        send(ref, ref, w_send, w_ring.at[h, way, d - 1, i], seq=ring_seq(h, sign))

    def arrived(h, way, d, i):
        sign = 1 if way == 0 else -1
        wait(ring_block(h, -sign * d, i), w_ring.at[h, way, d - 1, i])

    def exists(way, d, parity):
        return d < reach or (d == reach and parity == way)

    def weights_begin():
        def body(n, carry):
            ref = w_rows(0, y, z)
            send(ref, ref, w_send, w_first.at[0, n], seq=((y + n) % ny) * nz + z)
            ref = w_rows(1, y, z)
            send(ref, ref, w_send, w_first.at[1, n], seq=y * nz + (z + n) % nz)
            return carry

        lax.fori_loop(1, size, body, 0)

    def weights_first():
        def body(m, carry):
            for parity in range(2):
                i = 2 * m + parity
                for h in range(2):

                    def landed(i=i, h=h):
                        wait(ring_block(h, 0, i), w_first.at[h, i])

                    if parity == 0:
                        pl.when(m > 0)(landed)
                    else:
                        landed()
                    for way in range(2):
                        if exists(way, 1, parity):
                            pass_on(h, way, 1, i)
            return carry

        lax.fori_loop(0, size // 2, body, 0)

    def weights_step(d):
        def body(m, carry):
            for parity in range(2):
                i = 2 * m + parity
                for h in range(2):
                    for way in range(2):
                        if exists(way, d, parity):
                            arrived(h, way, d, i)
                            if exists(way, d + 1, parity):
                                pass_on(h, way, d + 1, i)
            return carry

        lax.fori_loop(0, size // 2, body, 0)

    def spread(src, dst, n):
        def body(i, carry):
            p = (s + i) % nseq
            send(src.at[p], dst.at[s], a2a_send.at[n], a2a_recv.at[n], seq=p)
            return carry

        lax.fori_loop(1, nseq, body, 0)
        dst[pl.ds(s, 1)] = src[pl.ds(s, 1)]

    def landed(dst, n):
        wait(dst.at[pl.ds(0, nseq - 1)], a2a_recv.at[n])

    mine = pl.multiple_of(s * block, block)
    wt[pl.ds(mine, block), :] = wgt[...].astype(F32).T.astype(BF16)
    weights_begin()

    out16[:, :GROUP, :] = sig[...].astype(F32).T.reshape(nseq, GROUP, LANES).astype(BF16)
    out16[:, GROUP:, :] = fil[...].astype(F32).T.reshape(nseq, GROUP, LANES).astype(BF16)
    spread(out16, in16, 0)

    call[c] = cot[...]
    send(call.at[c], call.at[c], c_send, c_recv.at[0], chan=sibling)
    for dx in range(1, nx):
        send(call.at[c], call.at[c], c_send, c_recv.at[dx], chan=x_peer(dx))

    weights_first()
    for dx in range(1, nx):
        ref = call.at[x_peer(-dx)]
        wait(ref, c_recv.at[dx])
        send(ref, ref, c_send, c_recv.at[nx - 1 + dx], chan=sibling)

    def by_channel(ref, width, start):
        return jnp.concatenate(
            [ref[pl.ds(start + n, nseq, stride=width), :] for n in range(GROUP)], axis=1
        )

    def to_blocks(ref, value, width, start):
        for n in range(GROUP):
            ref[pl.ds(start + n, nseq, stride=width), :] = value[:, n * LANES : (n + 1) * LANES]

    def gain(value):
        return jnp.concatenate(
            [
                value[:, n * LANES : (n + 1) * LANES] * skip[s * GROUP + n]
                for n in range(GROUP)
            ],
            axis=1,
        )

    weights_step(1)

    landed(in16, 0)
    rows32[...] = in16[...].astype(F32).reshape(nseq * 2 * GROUP, LANES)
    sig_x = by_channel(rows32, 2 * GROUP, 0)
    fil_x = by_channel(rows32, 2 * GROUP, GROUP)
    sf_spec[0] = forward(sig_x.astype(BF16), first, twist, second)
    sf_spec[1] = forward(fil_x.astype(BF16), first, twist, second)
    weights_step(2)
    conv = inverse(times(sf_spec[0], sf_spec[1]), twist, back, last)
    to_blocks(rows32, conv + gain(sig_x), GROUP, 0)
    out8[...] = rows32[pl.ds(0, nseq * GROUP), :].reshape(nseq, GROUP, LANES).astype(BF16)
    spread(out8, in8, 1)

    for d in range(3, reach + 1):
        weights_step(d)

    wait(call.at[sibling], c_recv.at[0])
    for dx in range(1, nx):
        wait(call.at[((x - dx) % nx) * CORES + (1 - core)], c_recv.at[nx - 1 + dx])
    total = jnp.zeros((LANES, chans), F32)
    for n in range(nx * CORES):
        total += mm(call[n], wt[pl.ds(n * chans, chans), :])
    grad[...] = total
    gates = gat[...].astype(F32)
    gconv = (total * gates).T
    gout8[...] = gconv.reshape(nseq, GROUP, LANES).astype(BF16)
    spread(gout8, gin8, 2)

    landed(in8, 1)
    before = in8[...].astype(F32).reshape(chans, LANES).T
    grad_gat[...] = (grad[...] * before).astype(BF16)
    gated = (before * gates).astype(BF16)

    def part(n):
        rows = wt[pl.ds(pl.multiple_of(n * chans, chans), chans), :]
        return lax.dot_general(
            gated, rows, (((1,), (1,)), ((), ())), preferred_element_type=F32
        )

    for n in range(nx):
        ex_out[n] = part(n * CORES + (1 - core)).astype(BF16)
        send(ex_out.at[n], ex_in.at[n], m_send.at[0], m_recv.at[n], chan=sibling)
    for n in range(nx):
        own[n] = part(n * CORES + core)

    landed(gin8, 2)
    rows32[pl.ds(0, nseq * GROUP), :] = gin8[...].astype(F32).reshape(nseq * GROUP, LANES)
    grad_x = by_channel(rows32, GROUP, 0)
    g_spec = forward(grad_x.astype(BF16), first, twist, second)
    through = inverse(times_conj(sf_spec[1], g_spec), twist, back, last)
    kern = inverse(times_conj(sf_spec[0], g_spec), twist, back, last)
    to_blocks(rows32, through + gain(grad_x), 2 * GROUP, 0)
    to_blocks(rows32, kern * (1.0 / math.sqrt(nseq * LANES)), 2 * GROUP, GROUP)
    rout16[...] = rows32[...].reshape(nseq, 2 * GROUP, LANES).astype(BF16)
    spread(rout16, rin16, 3)

    for n in range(nx):
        wait(ex_in.at[n], m_recv.at[n])
        own[n] += ex_in[n].astype(F32)
    for dx in range(1, nx):
        mx_out[dx - 1] = own[(x + dx) % nx].astype(BF16)
        send(mx_out.at[dx - 1], mx_in.at[dx - 1], m_send.at[1], m_recv.at[nx + dx], chan=x_peer(dx))
    result = own[x]
    for dx in range(1, nx):
        wait(mx_in.at[dx - 1], m_recv.at[nx + dx])
        result += mx_in[dx - 1].astype(F32)
    mixed[...] = result.astype(BF16)

    landed(rin16, 3)
    grads = rin16[...].astype(F32)
    grad_sig[...] = grads[:, :GROUP, :].reshape(chans, LANES).T.astype(BF16)
    grad_fil[...] = grads[:, GROUP:, :].reshape(chans, LANES).T.astype(BF16)

    for n, src in enumerate((out16, out8, gout8, rout16)):
        wait(src.at[pl.ds(0, nseq - 1)], a2a_send.at[n])
    wait(wt.at[pl.ds(0, (nseq - 1) * block)], w_send)
    wait(call.at[pl.ds(0, 2 * nx - 1)], c_send)
    wait(ex_out, m_send.at[0])
    wait(mx_out, m_send.at[1])


def local(ny, nz, nx, signal, gates, filters, skip_gain, out_proj, cotangent):
    nseq = ny * nz
    chans = signal.shape[1]
    block = out_proj.shape[1]
    first, twist, second, back, last = make_tables(nseq)
    rows = twist.shape[1]
    vmem = pl.BlockSpec(memory_space=pltpu.VMEM)
    smem = pl.BlockSpec(memory_space=pltpu.SMEM)
    out = jax.ShapeDtypeStruct((LANES, chans), BF16)
    wide = (nseq, 2 * GROUP, LANES)
    narrow = (nseq, GROUP, LANES)
    tile = (LANES, chans)
    return pl.pallas_call(
        functools.partial(kernel, ny, nz, nx),
        out_shape=[out] * 4,
        in_specs=[vmem, vmem, vmem, smem] + [vmem] * 7,
        out_specs=[vmem] * 4,
        scratch_shapes=[
            pltpu.VMEM(wide, BF16),
            pltpu.VMEM(wide, BF16),
            pltpu.VMEM(narrow, BF16),
            pltpu.VMEM(narrow, BF16),
            pltpu.VMEM(narrow, BF16),
            pltpu.VMEM(narrow, BF16),
            pltpu.VMEM(wide, BF16),
            pltpu.VMEM(wide, BF16),
            pltpu.VMEM((nseq * 2 * GROUP, LANES), F32),
            pltpu.VMEM((2, GROUP * rows, 2 * LANES), F32),
            pltpu.VMEM((nseq * block, chans), BF16),
            pltpu.VMEM((nx * CORES,) + tile, BF16),
            pltpu.VMEM(tile, F32),
            pltpu.VMEM((nx,) + tile, F32),
            pltpu.VMEM((nx,) + tile, BF16),
            pltpu.VMEM((nx,) + tile, BF16),
            pltpu.VMEM((nx - 1,) + tile, BF16),
            pltpu.VMEM((nx - 1,) + tile, BF16),
            pltpu.SemaphoreType.DMA((4,)),
            pltpu.SemaphoreType.DMA((4,)),
            pltpu.SemaphoreType.DMA,
            pltpu.SemaphoreType.DMA((2, ny)),
            pltpu.SemaphoreType.DMA((2, 2, ny // 2, ny)),
            pltpu.SemaphoreType.DMA,
            pltpu.SemaphoreType.DMA((2 * nx,)),
            pltpu.SemaphoreType.DMA((2,)),
            pltpu.SemaphoreType.DMA((2 * nx,)),
        ],
        compiler_params=pltpu.CompilerParams(
            collective_id=0, has_side_effects=True, vmem_limit_bytes=48 * 1024 * 1024
        ),
    )(signal, gates, filters, skip_gain, out_proj, cotangent, first, twist, second, back, last)


def solution(mesh):
    side = math.isqrt(mesh.shape["seq"])
    nx = mesh.shape["chan"] // CORES
    in_specs = (
        P("seq", "chan"),
        P("seq", "chan"),
        P("seq", "chan"),
        P("chan"),
        P("chan", "seq"),
        P("seq", "chan"),
    )
    out_specs = (P("seq", "chan"),) * 4
    return jax.shard_map(
        functools.partial(local, side, side, nx),
        mesh=mesh,
        in_specs=in_specs,
        out_specs=out_specs,
        check_vma=False,
    )
```

```python
import functools
import math

import jax
import jax.numpy as jnp
import ml_dtypes
import numpy as np
from jax import lax
from jax.experimental import pallas as pl
from jax.experimental.pallas import tpu as pltpu
from jax.sharding import PartitionSpec as P

LANES = 128
GROUP = 8
CORES = 2
MESH = pl.DeviceIdType.MESH
VMEM_LIMIT = 60 * 1024 * 1024
F32 = jnp.float32
BF16 = jnp.bfloat16


def halves(table):
    high = table.astype(ml_dtypes.bfloat16)
    low = (table - high.astype(np.float64)).astype(ml_dtypes.bfloat16)
    return high, low


def make_tables(blocks):
    total = 2 * blocks * LANES
    rows = -(-(blocks + 1) // 8) * 8
    k = np.arange(rows)
    j = np.arange(blocks)
    b = np.arange(LANES)
    live = (k <= blocks)[:, None].astype(np.float64)
    outer = 2 * np.pi * ((k[:, None] * j[None, :]) % (2 * blocks)) / (2 * blocks)
    first = np.concatenate([live * np.cos(outer), -live * np.sin(outer)], axis=0)
    twist = 2 * np.pi * k[:, None] * b[None, :] / total
    inner = 2 * np.pi * ((b[:, None] * b[None, :]) % LANES) / LANES
    cos, sin = np.cos(inner), np.sin(inner)
    second = np.block([[cos, -sin], [sin, cos]])
    weight = np.where((k == 0) | (k == blocks), 1.0, 2.0)[:, None] * live / total
    last = np.concatenate([weight * np.cos(outer), -weight * np.sin(outer)], axis=0).T
    return (
        np.concatenate(halves(first), axis=1),
        np.stack([np.cos(twist), -np.sin(twist)]).astype(np.float32),
        np.stack(halves(second)),
        np.stack(halves(second.T)),
        np.stack(halves(last)),
    )


def split(value):
    high = value.astype(BF16)
    return high, (value - high.astype(F32)).astype(BF16)


def mm(left, right):
    return jnp.dot(left, right, preferred_element_type=F32)


def forward(x, first, twist, second):
    rows = twist.shape[1]
    mid = mm(first[...], jnp.concatenate([x, x], axis=0))
    cos, sin = twist[0], twist[1]
    pieces = []
    for c in range(GROUP):
        re = mid[:rows, c * LANES : (c + 1) * LANES]
        im = mid[rows:, c * LANES : (c + 1) * LANES]
        pieces.append(jnp.concatenate([re * cos - im * sin, re * sin + im * cos], axis=1))
    high, low = split(jnp.concatenate(pieces, axis=0))
    return mm(high, second[0]) + mm(low, second[0]) + mm(high, second[1])


def inverse(spec, twist, back, last):
    rows = twist.shape[1]
    high, low = split(spec)
    mid = mm(high, back[0]) + mm(low, back[0]) + mm(high, back[1])
    cos, sin = twist[0], twist[1]
    pieces = []
    for c in range(GROUP):
        re = mid[c * rows : (c + 1) * rows, :LANES]
        im = mid[c * rows : (c + 1) * rows, LANES:]
        pieces.append(jnp.concatenate([re * cos + im * sin, im * cos - re * sin], axis=0))
    high, low = split(jnp.concatenate(pieces, axis=1))
    return mm(last[0], high) + mm(last[1], high) + mm(last[0], low)


def times(a, b):
    ar, ai, br, bi = a[:, :LANES], a[:, LANES:], b[:, :LANES], b[:, LANES:]
    return jnp.concatenate([ar * br - ai * bi, ar * bi + ai * br], axis=1)


def times_conj(a, b):
    ar, ai, br, bi = a[:, :LANES], a[:, LANES:], b[:, :LANES], b[:, LANES:]
    return jnp.concatenate([ar * br + ai * bi, ar * bi - ai * br], axis=1)


def kernel(
    ny,
    nz,
    nx,
    skip,
    sig_hbm,
    gat_hbm,
    fil_hbm,
    wgt_hbm,
    cot_hbm,
    first_hbm,
    twist_hbm,
    second_hbm,
    back_hbm,
    last_hbm,
    outs,
    sig,
    gat,
    fil,
    first,
    twist,
    second,
    back,
    last,
    load_sem,
    out16,
    in16,
    out8,
    in8,
    gout8,
    gin8,
    rout16,
    rin16,
    rows32,
    sf_spec,
    wt,
    call,
    grad,
    own,
    ex_out,
    ex_in,
    mx_out,
    mx_in,
    a2a_send,
    a2a_recv,
    w_send,
    w_first,
    w_ring,
    c_send,
    c_recv,
    m_send,
    m_recv,
    all_in,
):
    nseq = ny * nz
    chans = GROUP * nseq
    s = lax.axis_index("seq")
    c = lax.axis_index("chan")
    y, z = s // nz, s % nz
    x, core = c // CORES, c % CORES
    sibling = x * CORES + (1 - core)
    block = wgt_hbm.shape[0]
    half = block // 2

    def x_peer(dx):
        return ((x + dx) % nx) * CORES + core

    mine = pl.ds(pl.multiple_of(s * block, block), block)
    loads = [
        pltpu.make_async_copy(src, dst, load_sem.at[n])
        for n, (src, dst) in enumerate(
            (
                (wgt_hbm, wt.at[mine]),
                (sig_hbm, sig),
                (fil_hbm, fil),
                (cot_hbm, call.at[c]),
                (gat_hbm, gat),
                (first_hbm, first),
                (twist_hbm, twist),
                (second_hbm, second),
                (back_hbm, back),
                (last_hbm, last),
            )
        )
    ]
    for load in loads:
        load.start()

    bar = pltpu.get_barrier_semaphore()

    def row_peer(n):
        return y * nz + (z + n) % nz

    def column_peer(n):
        return ((y + n) % ny) * nz + z

    def greet(n, carry):
        for peer in (row_peer(n), column_peer(n)):
            pl.semaphore_signal(bar, inc=1, device_id={"seq": peer}, device_id_type=MESH)
        return carry

    lax.fori_loop(1, ny, greet, 0)
    for dx in range(1, nx):
        pl.semaphore_signal(bar, inc=1, device_id={"chan": x_peer(dx)}, device_id_type=MESH)
    pl.semaphore_signal(bar, inc=1, device_id={"chan": sibling}, device_id_type=MESH)
    pl.semaphore_wait(bar, ny + nz + nx - 2)

    def greet_all(n, carry):
        pl.semaphore_signal(
            all_in, inc=1, device_id={"seq": row_peer(n)}, device_id_type=MESH
        )
        return carry

    lax.fori_loop(1, nz, greet_all, 0)

    def send(src, dst, send_sem, recv_sem, **where):
        pltpu.make_async_remote_copy(
            src_ref=src,
            dst_ref=dst,
            send_sem=send_sem,
            recv_sem=recv_sem,
            device_id=where,
            device_id_type=MESH,
        ).start()

    def wait(ref, sem):
        pltpu.make_async_copy(ref, ref, sem).wait()

    def w_rows(h, yy, zz):
        start = pl.multiple_of((yy * nz + zz) * block + h * half, half)
        return wt.at[pl.ds(start, half)]

    def ring_seq(h, step):
        if h == 0:
            return y * nz + (z + step) % nz
        return ((y + step) % ny) * nz + z

    def ring_block(h, offset, i):
        if h == 0:
            return w_rows(0, (y - i) % ny, (z + offset) % nz)
        return w_rows(1, (y + offset) % ny, (z - i) % nz)

    size = ny
    reach = size // 2

    def pass_on(h, way, d, i):
        sign = 1 if way == 0 else -1
        ref = ring_block(h, -sign * (d - 1), i)
        send(ref, ref, w_send, w_ring.at[h, way, d - 1, i], seq=ring_seq(h, sign))

    def arrived(h, way, d, i):
        sign = 1 if way == 0 else -1
        wait(ring_block(h, -sign * d, i), w_ring.at[h, way, d - 1, i])

    def exists(way, d, parity):
        return d < reach or (d == reach and parity == way)

    def weights_begin():
        def body(n, carry):
            ref = w_rows(0, y, z)
            send(ref, ref, w_send, w_first.at[0, n], seq=((y + n) % ny) * nz + z)
            ref = w_rows(1, y, z)
            send(ref, ref, w_send, w_first.at[1, n], seq=y * nz + (z + n) % nz)
            return carry

        lax.fori_loop(1, size, body, 0)

    def weights_first():
        def body(m, carry):
            for parity in range(2):
                i = 2 * m + parity
                for h in range(2):

                    def landed(i=i, h=h):
                        wait(ring_block(h, 0, i), w_first.at[h, i])

                    if parity == 0:
                        pl.when(m > 0)(landed)
                    else:
                        landed()
                    for way in range(2):
                        if exists(way, 1, parity):
                            pass_on(h, way, 1, i)
            return carry

        lax.fori_loop(0, size // 2, body, 0)

    def weights_step(d):
        def body(m, carry):
            for parity in range(2):
                i = 2 * m + parity
                for h in range(2):
                    for way in range(2):
                        if exists(way, d, parity):
                            arrived(h, way, d, i)
                            if exists(way, d + 1, parity):
                                pass_on(h, way, d + 1, i)
            return carry

        lax.fori_loop(0, size // 2, body, 0)

    def spread(src, dst, n):
        def body(i, carry):
            p = (s + i) % nseq
            send(src.at[p], dst.at[s], a2a_send.at[n], a2a_recv.at[n], seq=p)
            return carry

        lax.fori_loop(1, nseq, body, 0)
        dst[pl.ds(s, 1)] = src[pl.ds(s, 1)]

    def landed(dst, n):
        wait(dst.at[pl.ds(0, nseq - 1)], a2a_recv.at[n])

    loads[0].wait()
    weights_begin()
    loads[1].wait()
    loads[2].wait()

    out16[:, :GROUP, :] = sig[...].astype(F32).T.reshape(nseq, GROUP, LANES).astype(BF16)
    out16[:, GROUP:, :] = fil[...].astype(F32).T.reshape(nseq, GROUP, LANES).astype(BF16)
    pl.semaphore_wait(all_in, nz - 1)
    spread(out16, in16, 0)

    loads[3].wait()
    send(call.at[c], call.at[c], c_send, c_recv.at[0], chan=sibling)
    for dx in range(1, nx):
        send(call.at[c], call.at[c], c_send, c_recv.at[dx], chan=x_peer(dx))

    for load in loads[4:]:
        load.wait()
    weights_first()
    for dx in range(1, nx):
        ref = call.at[x_peer(-dx)]
        wait(ref, c_recv.at[dx])
        send(ref, ref, c_send, c_recv.at[nx - 1 + dx], chan=sibling)

    def by_channel(ref, width, start):
        return jnp.concatenate(
            [ref[pl.ds(start + n, nseq, stride=width), :] for n in range(GROUP)], axis=1
        )

    def to_blocks(ref, value, width, start):
        for n in range(GROUP):
            ref[pl.ds(start + n, nseq, stride=width), :] = value[:, n * LANES : (n + 1) * LANES]

    def gain(value):
        return jnp.concatenate(
            [
                value[:, n * LANES : (n + 1) * LANES] * skip[s * GROUP + n]
                for n in range(GROUP)
            ],
            axis=1,
        )

    weights_step(1)

    landed(in16, 0)
    rows32[...] = in16[...].astype(F32).reshape(nseq * 2 * GROUP, LANES)
    sig_x = by_channel(rows32, 2 * GROUP, 0)
    fil_x = by_channel(rows32, 2 * GROUP, GROUP)
    sf_spec[0] = forward(sig_x.astype(BF16), first, twist, second)
    sf_spec[1] = forward(fil_x.astype(BF16), first, twist, second)
    weights_step(2)
    conv = inverse(times(sf_spec[0], sf_spec[1]), twist, back, last)
    to_blocks(rows32, conv + gain(sig_x), GROUP, 0)
    out8[...] = rows32[pl.ds(0, nseq * GROUP), :].reshape(nseq, GROUP, LANES).astype(BF16)
    spread(out8, in8, 1)

    for d in range(3, reach + 1):
        weights_step(d)

    wait(call.at[sibling], c_recv.at[0])
    for dx in range(1, nx):
        wait(call.at[((x - dx) % nx) * CORES + (1 - core)], c_recv.at[nx - 1 + dx])
    total = jnp.zeros((LANES, chans), F32)
    for n in range(nx * CORES):
        total += mm(call[n], wt[pl.ds(n * chans, chans), :])
    grad[...] = total
    gates = gat[...].astype(F32)
    gconv = (total * gates).T
    gout8[...] = gconv.reshape(nseq, GROUP, LANES).astype(BF16)
    spread(gout8, gin8, 2)

    landed(in8, 1)
    before = in8[...].astype(F32).reshape(chans, LANES).T
    outs[2] = (grad[...] * before).astype(BF16)
    gated = (before * gates).astype(BF16)

    def part(n):
        rows = wt[pl.ds(pl.multiple_of(n * chans, chans), chans), :]
        return lax.dot_general(
            gated, rows, (((1,), (1,)), ((), ())), preferred_element_type=F32
        )

    for n in range(nx):
        ex_out[n] = part(n * CORES + (1 - core)).astype(BF16)
        send(ex_out.at[n], ex_in.at[n], m_send.at[0], m_recv.at[n], chan=sibling)
    for n in range(nx):
        own[n] = part(n * CORES + core)

    landed(gin8, 2)
    rows32[pl.ds(0, nseq * GROUP), :] = gin8[...].astype(F32).reshape(nseq * GROUP, LANES)
    grad_x = by_channel(rows32, GROUP, 0)
    g_spec = forward(grad_x.astype(BF16), first, twist, second)
    through = inverse(times_conj(sf_spec[1], g_spec), twist, back, last)
    kern = inverse(times_conj(sf_spec[0], g_spec), twist, back, last)
    to_blocks(rows32, through + gain(grad_x), 2 * GROUP, 0)
    to_blocks(rows32, kern * (1.0 / math.sqrt(nseq * LANES)), 2 * GROUP, GROUP)
    rout16[...] = rows32[...].reshape(nseq, 2 * GROUP, LANES).astype(BF16)
    spread(rout16, rin16, 3)

    for n in range(nx):
        wait(ex_in.at[n], m_recv.at[n])
        own[n] += ex_in[n].astype(F32)
    for dx in range(1, nx):
        mx_out[dx - 1] = own[(x + dx) % nx].astype(BF16)
        send(mx_out.at[dx - 1], mx_in.at[dx - 1], m_send.at[1], m_recv.at[nx + dx], chan=x_peer(dx))
    result = own[x]
    for dx in range(1, nx):
        wait(mx_in.at[dx - 1], m_recv.at[nx + dx])
        result += mx_in[dx - 1].astype(F32)
    outs[0] = result.astype(BF16)

    landed(rin16, 3)
    grads = rin16[...].astype(F32)
    outs[1] = grads[:, :GROUP, :].reshape(chans, LANES).T.astype(BF16)
    outs[3] = grads[:, GROUP:, :].reshape(chans, LANES).T.astype(BF16)

    for n, src in enumerate((out16, out8, gout8, rout16)):
        wait(src.at[pl.ds(0, nseq - 1)], a2a_send.at[n])
    wait(wt.at[pl.ds(0, (nseq - 1) * block)], w_send)
    wait(call.at[pl.ds(0, 2 * nx - 1)], c_send)
    wait(ex_out, m_send.at[0])
    wait(mx_out, m_send.at[1])


def local(ny, nz, nx, signal, gates, filters, skip_gain, out_proj, cotangent):
    nseq = ny * nz
    chans = signal.shape[1]
    block = out_proj.shape[1]
    first, twist, second, back, last = make_tables(nseq)
    rows = twist.shape[1]
    hbm = pl.BlockSpec(memory_space=pltpu.HBM)
    vmem = pl.BlockSpec(memory_space=pltpu.VMEM)
    smem = pl.BlockSpec(memory_space=pltpu.SMEM)
    out = jax.ShapeDtypeStruct((LANES, chans), BF16)
    wide = (nseq, 2 * GROUP, LANES)
    narrow = (nseq, GROUP, LANES)
    tile = (LANES, chans)
    results = pl.pallas_call(
        functools.partial(kernel, ny, nz, nx),
        out_shape=jax.ShapeDtypeStruct((4, LANES, chans), BF16),
        in_specs=[smem] + [hbm] * 10,
        out_specs=vmem,
        scratch_shapes=[
            pltpu.VMEM(tile, BF16),
            pltpu.VMEM(tile, BF16),
            pltpu.VMEM(tile, BF16),
            pltpu.VMEM(first.shape, BF16),
            pltpu.VMEM(twist.shape, F32),
            pltpu.VMEM(second.shape, BF16),
            pltpu.VMEM(back.shape, BF16),
            pltpu.VMEM(last.shape, BF16),
            pltpu.SemaphoreType.DMA((10,)),
            pltpu.VMEM(wide, BF16),
            pltpu.VMEM(wide, BF16),
            pltpu.VMEM(narrow, BF16),
            pltpu.VMEM(narrow, BF16),
            pltpu.VMEM(narrow, BF16),
            pltpu.VMEM(narrow, BF16),
            pltpu.VMEM(wide, BF16),
            pltpu.VMEM(wide, BF16),
            pltpu.VMEM((nseq * 2 * GROUP, LANES), F32),
            pltpu.VMEM((2, GROUP * rows, 2 * LANES), F32),
            pltpu.VMEM((nseq * block, chans), BF16),
            pltpu.VMEM((nx * CORES,) + tile, BF16),
            pltpu.VMEM(tile, F32),
            pltpu.VMEM((nx,) + tile, F32),
            pltpu.VMEM((nx,) + tile, BF16),
            pltpu.VMEM((nx,) + tile, BF16),
            pltpu.VMEM((nx - 1,) + tile, BF16),
            pltpu.VMEM((nx - 1,) + tile, BF16),
            pltpu.SemaphoreType.DMA((4,)),
            pltpu.SemaphoreType.DMA((4,)),
            pltpu.SemaphoreType.DMA,
            pltpu.SemaphoreType.DMA((2, ny)),
            pltpu.SemaphoreType.DMA((2, 2, ny // 2, ny)),
            pltpu.SemaphoreType.DMA,
            pltpu.SemaphoreType.DMA((2 * nx,)),
            pltpu.SemaphoreType.DMA((2,)),
            pltpu.SemaphoreType.DMA((2 * nx,)),
            pltpu.SemaphoreType.REGULAR,
        ],
        compiler_params=pltpu.CompilerParams(
            collective_id=0, has_side_effects=True, vmem_limit_bytes=VMEM_LIMIT
        ),
    )(
        skip_gain,
        signal,
        gates,
        filters,
        out_proj.T,
        cotangent,
        first,
        twist,
        second,
        back,
        last,
    )
    return tuple(results[n] for n in range(4))


def solution(mesh):
    side = math.isqrt(mesh.shape["seq"])
    nx = mesh.shape["chan"] // CORES
    in_specs = (
        P("seq", "chan"),
        P("seq", "chan"),
        P("seq", "chan"),
        P("chan"),
        P("chan", "seq"),
        P("seq", "chan"),
    )
    out_specs = (P("seq", "chan"),) * 4
    return jax.shard_map(
        functools.partial(local, side, side, nx),
        mesh=mesh,
        in_specs=in_specs,
        out_specs=out_specs,
        check_vma=False,
    )
```

```python
import functools
import math

import jax
import jax.numpy as jnp
import ml_dtypes
import numpy as np
from jax import lax
from jax.experimental import pallas as pl
from jax.experimental.pallas import tpu as pltpu
from jax.sharding import PartitionSpec as P

LANES = 128
GROUP = 8
CORES = 2
MESH = pl.DeviceIdType.MESH
VMEM_LIMIT = 60 * 1024 * 1024
F32 = jnp.float32
BF16 = jnp.bfloat16


def halves(table):
    high = table.astype(ml_dtypes.bfloat16)
    low = (table - high.astype(np.float64)).astype(ml_dtypes.bfloat16)
    return high, low


def make_tables(blocks):
    total = 2 * blocks * LANES
    rows = -(-(blocks + 1) // 8) * 8
    k = np.arange(rows)
    j = np.arange(blocks)
    b = np.arange(LANES)
    live = (k <= blocks)[:, None].astype(np.float64)
    outer = 2 * np.pi * ((k[:, None] * j[None, :]) % (2 * blocks)) / (2 * blocks)
    first = np.concatenate([live * np.cos(outer), -live * np.sin(outer)], axis=0)
    twist = 2 * np.pi * k[:, None] * b[None, :] / total
    inner = 2 * np.pi * ((b[:, None] * b[None, :]) % LANES) / LANES
    cos, sin = np.cos(inner), np.sin(inner)
    second = np.block([[cos, -sin], [sin, cos]])
    weight = np.where((k == 0) | (k == blocks), 1.0, 2.0)[:, None] * live / total
    last = np.concatenate([weight * np.cos(outer), -weight * np.sin(outer)], axis=0).T
    return (
        np.concatenate(halves(first), axis=1),
        np.stack([np.cos(twist), -np.sin(twist)]).astype(np.float32),
        np.stack(halves(second)),
        np.stack(halves(second.T)),
        np.stack(halves(last)),
    )


def split(value):
    high = value.astype(BF16)
    return high, (value - high.astype(F32)).astype(BF16)


def mm(left, right):
    return jnp.dot(left, right, preferred_element_type=F32)


def forward(x, first, twist, second):
    rows = twist.shape[1]
    mid = mm(first[...], jnp.concatenate([x, x], axis=0))
    cos, sin = twist[0], twist[1]
    pieces = []
    for c in range(GROUP):
        re = mid[:rows, c * LANES : (c + 1) * LANES]
        im = mid[rows:, c * LANES : (c + 1) * LANES]
        pieces.append(jnp.concatenate([re * cos - im * sin, re * sin + im * cos], axis=1))
    high, low = split(jnp.concatenate(pieces, axis=0))
    return mm(high, second[0]) + mm(low, second[0]) + mm(high, second[1])


def inverse(spec, twist, back, last):
    rows = twist.shape[1]
    high, low = split(spec)
    mid = mm(high, back[0]) + mm(low, back[0]) + mm(high, back[1])
    cos, sin = twist[0], twist[1]
    pieces = []
    for c in range(GROUP):
        re = mid[c * rows : (c + 1) * rows, :LANES]
        im = mid[c * rows : (c + 1) * rows, LANES:]
        pieces.append(jnp.concatenate([re * cos + im * sin, im * cos - re * sin], axis=0))
    high, low = split(jnp.concatenate(pieces, axis=1))
    return mm(last[0], high) + mm(last[1], high) + mm(last[0], low)


def times(a, b):
    ar, ai, br, bi = a[:, :LANES], a[:, LANES:], b[:, :LANES], b[:, LANES:]
    return jnp.concatenate([ar * br - ai * bi, ar * bi + ai * br], axis=1)


def times_conj(a, b):
    ar, ai, br, bi = a[:, :LANES], a[:, LANES:], b[:, :LANES], b[:, LANES:]
    return jnp.concatenate([ar * br + ai * bi, ar * bi - ai * br], axis=1)


def kernel(
    ny,
    nz,
    nx,
    skip,
    sig_hbm,
    gat_hbm,
    fil_hbm,
    wgt_hbm,
    cot_hbm,
    first_hbm,
    twist_hbm,
    second_hbm,
    back_hbm,
    last_hbm,
    outs,
    sig,
    gat,
    fil,
    first,
    twist,
    second,
    back,
    last,
    load_sem,
    out16,
    in16,
    out8,
    in8,
    gout8,
    gin8,
    rout16,
    rin16,
    rows32,
    sf_spec,
    wt,
    order,
    cot_own,
    cot_perm,
    ck0,
    ck1,
    gp_out,
    gp_in,
    gated,
    own0,
    own1,
    ex0_out,
    ex0_in,
    ex1_out,
    ex1_in,
    mx0_out,
    mx0_in,
    mx1_out,
    mx1_in,
    ret0_out,
    ret0_in,
    ret1_out,
    ret1_in,
    perm,
    gating,
    a2a_send,
    a2a_recv,
    w_send,
    w_first,
    w_ring,
    k0_send,
    k0_recv,
    k1_send,
    k1_recv,
    p_send,
    p_recv,
    m0_send,
    m0_recv,
    m1_send,
    m1_recv,
    all_in,
):
    nseq = ny * nz
    chans = GROUP * nseq
    s = lax.axis_index("seq")
    c = lax.axis_index("chan")
    y, z = s // nz, s % nz
    x, core = c // CORES, c % CORES
    sibling = x * CORES + (1 - core)
    block = wgt_hbm.shape[0]
    half = block // 2
    quarter = chans // 4
    middle = chans // 2
    pz, py = z % 2, y % 2
    z_pair = y * nz + (z + 1 - 2 * pz)
    y_pair = (y + 1 - 2 * py) * nz + z
    keeps = core == py
    hop = ny // 2
    base = nseq * half // 2

    def cols0(n):
        return pl.ds(pl.multiple_of(n * quarter, quarter), quarter)

    def cols1(n):
        return pl.ds(pl.multiple_of(n * middle, middle), middle)

    def x_peer(dx):
        return ((x + dx) % nx) * CORES + core

    def w_rows(h, a, b):
        width = nz // 2 if h == 0 else nz
        start = pl.multiple_of(h * base + (a * width + b) * half, half)
        return wt.at[pl.ds(start, half)]

    def held(h, i, d):
        if h == 0:
            return w_rows(0, (y - d) % ny, (z // 2 - i) % hop)
        return w_rows(1, (y // 2 - i) % hop, (z - d) % nz)

    loads = [
        pltpu.make_async_copy(src, dst, load_sem.at[n])
        for n, (src, dst) in enumerate(
            (
                (wgt_hbm.at[pl.ds(0, half)], held(0, 0, 0)),
                (wgt_hbm.at[pl.ds(half, half)], held(1, 0, 0)),
                (cot_hbm, cot_own),
                (sig_hbm, sig),
                (fil_hbm, fil),
                (gat_hbm, gat),
                (first_hbm, first),
                (twist_hbm, twist),
                (second_hbm, second),
                (back_hbm, back),
                (last_hbm, last),
            )
        )
    ]
    for load in loads:
        load.start()

    bar = pltpu.get_barrier_semaphore()

    def row_peer(n):
        return y * nz + (z + n) % nz

    def column_peer(n):
        return ((y + n) % ny) * nz + z

    def greet(n, carry):
        for peer in (row_peer(n), column_peer(n)):
            pl.semaphore_signal(bar, inc=1, device_id={"seq": peer}, device_id_type=MESH)
        return carry

    lax.fori_loop(1, ny, greet, 0)
    for dx in range(1, nx):
        pl.semaphore_signal(bar, inc=1, device_id={"chan": x_peer(dx)}, device_id_type=MESH)
    pl.semaphore_signal(bar, inc=1, device_id={"chan": sibling}, device_id_type=MESH)

    loads[3].wait()
    loads[4].wait()
    out16[:, :GROUP, :] = sig[...].astype(F32).T.reshape(nseq, GROUP, LANES).astype(BF16)
    out16[:, GROUP:, :] = fil[...].astype(F32).T.reshape(nseq, GROUP, LANES).astype(BF16)
    column = lax.broadcasted_iota(jnp.int32, (chans, chans), 0)
    place = lax.broadcasted_iota(jnp.int32, (chans, chans), 1)
    zz = column // block
    rest = column % block
    target = jnp.where(
        rest < half,
        (zz % 2) * quarter + (zz // 2) * half + rest,
        middle + zz * half + rest - half,
    )
    order[...] = (place == target).astype(F32).astype(BF16)
    loads[2].wait()
    cot_perm[...] = mm(cot_own[...], order[...]).astype(BF16)
    near = pl.ds(pl.multiple_of(pz * quarter, quarter), quarter)
    far = pl.ds(pl.multiple_of((1 - pz) * quarter, quarter), quarter)
    ck0[0, :, cols0(c)] = cot_perm[:, near]

    @pl.when(keeps)
    def _():
        ck1[0, :, cols1(x)] = cot_perm[:, middle:]

    pl.semaphore_wait(bar, ny + nz + nx - 2)

    def greet_all(n, carry):
        pl.semaphore_signal(
            all_in, inc=1, device_id={"seq": row_peer(n)}, device_id_type=MESH
        )
        return carry

    lax.fori_loop(1, nz, greet_all, 0)

    def send(src, dst, send_sem, recv_sem, **where):
        pltpu.make_async_remote_copy(
            src_ref=src,
            dst_ref=dst,
            send_sem=send_sem,
            recv_sem=recv_sem,
            device_id=where,
            device_id_type=MESH,
        ).start()

    def wait(ref, sem):
        pltpu.make_async_copy(ref, ref, sem).wait()

    reach = ny // 2

    def beside(h, way):
        step = 1 - 2 * way
        return column_peer(step) if h == 0 else row_peer(step)

    def pass_on(h, way, d, i):
        sign = 1 - 2 * way
        ref = held(h, i, sign * (d - 1))
        send(ref, ref, w_send, w_ring.at[h, way, d - 1, i], seq=beside(h, way))

    def exists(way, d, parity):
        return d < reach or (d == reach and parity == way)

    def weights_begin():
        def body(n, carry):
            ref = held(0, 0, 0)
            send(ref, ref, w_send, w_first.at[0, n], seq=row_peer(2 * n))
            ref = held(1, 0, 0)
            send(ref, ref, w_send, w_first.at[1, n], seq=column_peer(2 * n))
            return carry

        lax.fori_loop(1, hop, body, 0)
        for h in range(2):
            for way in range(2):
                if exists(way, 1, 0):
                    pass_on(h, way, 1, 0)

    def weights_first(i):
        for h in range(2):
            wait(held(h, i, 0), w_first.at[h, i])
            for way in range(2):
                if exists(way, 1, i % 2):
                    pass_on(h, way, 1, i)

    def weights_step(d, i):
        for h in range(2):
            for way in range(2):
                if exists(way, d, i % 2):
                    wait(held(h, i, (1 - 2 * way) * d), w_ring.at[h, way, d - 1, i])
                    if exists(way, d + 1, i % 2):
                        pass_on(h, way, d + 1, i)

    def spread(src, dst, n, first_peer=1, end=nseq):
        def body(i, carry):
            p = (s + i) % nseq
            send(src.at[p], dst.at[s], a2a_send.at[n], a2a_recv.at[n], seq=p)
            return carry

        lax.fori_loop(first_peer, end, body, 0)
        if first_peer == 1:
            dst[pl.ds(s, 1)] = src[pl.ds(s, 1)]

    def spread_part(src, dst, n, part):
        piece = nseq // 4
        spread(src, dst, n, max(1, part * piece), (part + 1) * piece)

    def landed(dst, n):
        wait(dst.at[pl.ds(0, nseq - 1)], a2a_recv.at[n])

    def by_channel(ref, width, start):
        return jnp.concatenate(
            [ref[pl.ds(start + n, nseq, stride=width), :] for n in range(GROUP)], axis=1
        )

    def to_blocks(ref, value, width, start):
        for n in range(GROUP):
            ref[pl.ds(start + n, nseq, stride=width), :] = value[:, n * LANES : (n + 1) * LANES]

    def gain(value):
        return jnp.concatenate(
            [
                value[:, n * LANES : (n + 1) * LANES] * skip[s * GROUP + n]
                for n in range(GROUP)
            ],
            axis=1,
        )


    def to_all(ref, send_sem, recv_sem):
        send(ref, ref, send_sem.at[0], recv_sem.at[0], chan=sibling)
        for dx in range(1, nx):
            send(ref, ref, send_sem.at[dx], recv_sem.at[dx], chan=x_peer(dx))

    def cotangent_out():
        ref = ck0.at[1, :, cols0(c)]
        wait(ref, p_recv.at[0])
        to_all(ck0.at[:, :, cols0(c)], k0_send, k0_recv)

        @pl.when(keeps)
        def _():
            wait(ck1.at[1, :, cols1(x)], p_recv.at[1])
            to_all(ck1.at[:, :, cols1(x)], k1_send, k1_recv)

    def cotangent_on():
        for dx in range(1, nx):
            ref = ck0.at[:, :, cols0(x_peer(-dx))]
            wait(ref, k0_recv.at[dx])
            send(ref, ref, k0_send.at[nx - 1 + dx], k0_recv.at[nx - 1 + dx], chan=sibling)

        @pl.when(keeps)
        def _():
            for dx in range(1, nx):
                ref = ck1.at[:, :, cols1((x - dx) % nx)]
                wait(ref, k1_recv.at[dx])
                send(ref, ref, k1_send.at[nx - 1 + dx], k1_recv.at[nx - 1 + dx], chan=sibling)

    def cotangent_in():
        wait(ck0.at[:, :, cols0(sibling)], k0_recv.at[0])
        for dx in range(1, nx):
            other = ((x - dx) % nx) * CORES + (1 - core)
            wait(ck0.at[:, :, cols0(other)], k0_recv.at[nx - 1 + dx])

        @pl.when(jnp.logical_not(keeps))
        def _():
            wait(ck1.at[:, :, cols1(x)], k1_recv.at[0])
            for dx in range(1, nx):
                wait(ck1.at[:, :, cols1((x - dx) % nx)], k1_recv.at[nx - 1 + dx])

    def tokens_out(part):
        if part == 0:
            pl.semaphore_wait(all_in, nz - 1)
        spread_part(out16, in16, 0, part)

    def transform(n):
        if n == 0:
            landed(in16, 0)
            rows32[...] = in16[...].astype(F32).reshape(nseq * 2 * GROUP, LANES)
            for load in loads[5:]:
                load.wait()
        value = by_channel(rows32, 2 * GROUP, n * GROUP)
        sf_spec[n] = forward(value.astype(BF16), first, twist, second)

    def convolve():
        value = inverse(times(sf_spec[0], sf_spec[1]), twist, back, last)
        value += gain(by_channel(rows32, 2 * GROUP, 0))
        to_blocks(rows32, value, GROUP, 0)
        out8[...] = rows32[pl.ds(0, nseq * GROUP), :].reshape(nseq, GROUP, LANES).astype(BF16)

    def before_out(part):
        spread_part(out8, in8, 1, part)

    def gate():
        landed(in8, 1)
        gating[...] = in8[...].astype(F32).reshape(chans, LANES).T
        gated[0] = (gating[...] * gat[...].astype(F32)).astype(BF16)

    def gate_out():
        send(gated.at[0], gated.at[1], p_send.at[4], p_recv.at[4], seq=z_pair)
        send(gated.at[0], gated.at[2], p_send.at[5], p_recv.at[5], seq=y_pair)

    loads[0].wait()
    loads[1].wait()
    weights_begin()
    send(cot_perm.at[:, far], ck0.at[1, :, cols0(c)], p_send.at[0], p_recv.at[0], seq=z_pair)

    @pl.when(jnp.logical_not(keeps))
    def _():
        send(
            cot_perm.at[:, pl.ds(middle, middle)],
            ck1.at[1, :, cols1(x)],
            p_send.at[1],
            p_recv.at[1],
            seq=y_pair,
        )

    weights_first(1)
    tokens_out(0)
    weights_first(2)
    tokens_out(1)
    weights_first(3)
    tokens_out(2)
    weights_step(1, 0)
    tokens_out(3)
    weights_step(1, 1)
    cotangent_out()
    weights_step(1, 2)
    weights_step(1, 3)
    weights_step(2, 0)
    cotangent_on()
    weights_step(2, 1)
    weights_step(2, 2)
    transform(0)
    weights_step(2, 3)
    transform(1)
    weights_step(3, 0)
    convolve()
    weights_step(3, 1)
    before_out(0)
    weights_step(3, 2)
    before_out(1)
    weights_step(3, 3)
    before_out(2)
    weights_step(4, 0)
    before_out(3)
    cotangent_in()
    weights_step(4, 1)
    weights_step(4, 2)
    weights_step(4, 3)
    sum0 = mm(ck0[...].reshape(2 * LANES, -1), wt[pl.ds(0, base), :])
    gp_out[0] = sum0[LANES:].astype(BF16)
    send(gp_out.at[0], gp_in.at[0], p_send.at[2], p_recv.at[2], seq=z_pair)
    sum1 = mm(ck1[...].reshape(2 * LANES, -1), wt[pl.ds(base, base), :])
    gp_out[1] = sum1[LANES:].astype(BF16)
    send(gp_out.at[1], gp_in.at[1], p_send.at[3], p_recv.at[3], seq=y_pair)

    gate()
    gate_out()
    mine = sum0[:LANES] + sum1[:LANES]
    wait(gp_in.at[0], p_recv.at[2])
    wait(gp_in.at[1], p_recv.at[3])
    gates = gat[...].astype(F32)
    total = mine + gp_in[0].astype(F32) + gp_in[1].astype(F32)
    gconv = (total * gates).T
    gout8[...] = gconv.reshape(nseq, GROUP, LANES).astype(BF16)
    spread(gout8, gin8, 2)
    outs[2] = (total * gating[...]).astype(BF16)

    wait(gated.at[1], p_recv.at[4])
    wait(gated.at[2], p_recv.at[5])

    def part(tokens, start, width):
        return lax.dot_general(
            tokens,
            wt[pl.ds(pl.multiple_of(start, width), width), :],
            (((1,), (1,)), ((), ())),
            preferred_element_type=F32,
        )

    z_tokens = jnp.concatenate([gated[0], gated[1]], axis=0)
    y_tokens = jnp.concatenate([gated[0], gated[2]], axis=0)

    def part0(n):
        return part(z_tokens, n * quarter, quarter)

    def part1(n):
        return part(y_tokens, base + n * middle, middle)

    for n in range(nx):
        ex0_out[n] = part0(n * CORES + (1 - core)).astype(BF16)
    send(ex0_out, ex0_in, m0_send.at[0], m0_recv.at[0], chan=sibling)

    @pl.when(jnp.logical_not(keeps))
    def _():
        for n in range(nx):
            ex1_out[n] = part1(n).astype(BF16)
        send(ex1_out, ex1_in, m1_send.at[0], m1_recv.at[0], chan=sibling)

    for n in range(nx):
        own0[n] = part0(n * CORES + core)

    @pl.when(keeps)
    def _():
        for n in range(nx):
            own1[n] = part1(n)
        wait(ex1_in, m1_recv.at[0])
        own1[...] += ex1_in[...].astype(F32)
        for dx in range(1, nx):
            mx1_out[dx - 1] = own1[(x + dx) % nx].astype(BF16)
            send(
                mx1_out.at[dx - 1],
                mx1_in.at[dx - 1],
                m1_send.at[dx],
                m1_recv.at[dx],
                chan=x_peer(dx),
            )

    wait(ex0_in, m0_recv.at[0])
    own0[...] += ex0_in[...].astype(F32)
    for dx in range(1, nx):
        mx0_out[dx - 1] = own0[(x + dx) % nx].astype(BF16)
        send(
            mx0_out.at[dx - 1],
            mx0_in.at[dx - 1],
            m0_send.at[dx],
            m0_recv.at[dx],
            chan=x_peer(dx),
        )

    landed(gin8, 2)
    rows32[pl.ds(0, nseq * GROUP), :] = gin8[...].astype(F32).reshape(nseq * GROUP, LANES)
    grad_x = by_channel(rows32, GROUP, 0)
    g_spec = forward(grad_x.astype(BF16), first, twist, second)
    through = inverse(times_conj(sf_spec[1], g_spec), twist, back, last)
    kern = inverse(times_conj(sf_spec[0], g_spec), twist, back, last)
    to_blocks(rows32, through + gain(grad_x), 2 * GROUP, 0)
    to_blocks(rows32, kern * (1.0 / math.sqrt(nseq * LANES)), 2 * GROUP, GROUP)
    rout16[...] = rows32[...].reshape(nseq, 2 * GROUP, LANES).astype(BF16)
    spread(rout16, rin16, 3)

    @pl.when(keeps)
    def _():
        result = own1[x]
        for dx in range(1, nx):
            wait(mx1_in.at[dx - 1], m1_recv.at[dx])
            result += mx1_in[dx - 1].astype(F32)
        perm[:, middle:] = result[:LANES].astype(BF16)
        ret1_out[...] = result[LANES:].astype(BF16)
        send(ret1_out, ret1_in, p_send.at[7], p_recv.at[7], seq=y_pair)

    result = own0[x]
    for dx in range(1, nx):
        wait(mx0_in.at[dx - 1], m0_recv.at[dx])
        result += mx0_in[dx - 1].astype(F32)
    perm[:, near] = result[:LANES].astype(BF16)
    ret0_out[...] = result[LANES:].astype(BF16)
    send(ret0_out, ret0_in, p_send.at[6], p_recv.at[6], seq=z_pair)

    wait(ret0_in, p_recv.at[6])
    perm[:, far] = ret0_in[...]

    @pl.when(jnp.logical_not(keeps))
    def _():
        wait(ret1_in, p_recv.at[7])
        perm[:, middle:] = ret1_in[...]

    outs[0] = lax.dot_general(
        perm[...], order[...], (((1,), (1,)), ((), ())), preferred_element_type=F32
    ).astype(BF16)

    landed(rin16, 3)
    grads = rin16[...].astype(F32)
    outs[1] = grads[:, :GROUP, :].reshape(chans, LANES).T.astype(BF16)
    outs[3] = grads[:, GROUP:, :].reshape(chans, LANES).T.astype(BF16)

    for n, src in enumerate((out16, out8, gout8, rout16)):
        wait(src.at[pl.ds(0, nseq - 1)], a2a_send.at[n])
    wait(wt.at[pl.ds(0, (2 * (hop - 1) + 2 * hop * (2 * reach - 1)) * half)], w_send)
    for n in range(2 * nx - 1):
        wait(ck0.at[:, :, cols0(0)], k0_send.at[n])
    wait(ck0.at[1, :, cols0(0)], p_send.at[0])
    wait(gp_out.at[0], p_send.at[2])
    wait(gp_out.at[1], p_send.at[3])
    wait(gated.at[0], p_send.at[4])
    wait(gated.at[0], p_send.at[5])
    wait(ret0_out, p_send.at[6])
    wait(ex0_out, m0_send.at[0])
    for dx in range(1, nx):
        wait(mx0_out.at[dx - 1], m0_send.at[dx])

    @pl.when(keeps)
    def _():
        for n in range(2 * nx - 1):
            wait(ck1.at[:, :, cols1(0)], k1_send.at[n])
        for dx in range(1, nx):
            wait(mx1_out.at[dx - 1], m1_send.at[dx])
        wait(ret1_out, p_send.at[7])

    @pl.when(jnp.logical_not(keeps))
    def _():
        wait(ck1.at[1, :, cols1(0)], p_send.at[1])
        wait(ex1_out, m1_send.at[0])


def local(ny, nz, nx, signal, gates, filters, skip_gain, out_proj, cotangent):
    nseq = ny * nz
    chans = signal.shape[1]
    half = out_proj.shape[1] // 2
    quarter, middle = chans // 4, chans // 2
    hop = ny // 2
    first, twist, second, back, last = make_tables(nseq)
    rows = twist.shape[1]
    hbm = pl.BlockSpec(memory_space=pltpu.HBM)
    vmem = pl.BlockSpec(memory_space=pltpu.VMEM)
    smem = pl.BlockSpec(memory_space=pltpu.SMEM)
    out = jax.ShapeDtypeStruct((LANES, chans), BF16)
    wide = (nseq, 2 * GROUP, LANES)
    narrow = (nseq, GROUP, LANES)
    tile = (LANES, chans)
    results = pl.pallas_call(
        functools.partial(kernel, ny, nz, nx),
        out_shape=jax.ShapeDtypeStruct((4, LANES, chans), BF16),
        in_specs=[smem] + [hbm] * 10,
        out_specs=vmem,
        scratch_shapes=[
            pltpu.VMEM(tile, BF16),
            pltpu.VMEM(tile, BF16),
            pltpu.VMEM(tile, BF16),
            pltpu.VMEM(first.shape, BF16),
            pltpu.VMEM(twist.shape, F32),
            pltpu.VMEM(second.shape, BF16),
            pltpu.VMEM(back.shape, BF16),
            pltpu.VMEM(last.shape, BF16),
            pltpu.SemaphoreType.DMA((11,)),
            pltpu.VMEM(wide, BF16),
            pltpu.VMEM(wide, BF16),
            pltpu.VMEM(narrow, BF16),
            pltpu.VMEM(narrow, BF16),
            pltpu.VMEM(narrow, BF16),
            pltpu.VMEM(narrow, BF16),
            pltpu.VMEM(wide, BF16),
            pltpu.VMEM(wide, BF16),
            pltpu.VMEM((nseq * 2 * GROUP, LANES), F32),
            pltpu.VMEM((2, GROUP * rows, 2 * LANES), F32),
            pltpu.VMEM((nseq * half, chans), BF16),
            pltpu.VMEM((chans, chans), BF16),
            pltpu.VMEM(tile, BF16),
            pltpu.VMEM(tile, BF16),
            pltpu.VMEM((2, LANES, nx * CORES * quarter), BF16),
            pltpu.VMEM((2, LANES, nx * middle), BF16),
            pltpu.VMEM((2,) + tile, BF16),
            pltpu.VMEM((2,) + tile, BF16),
            pltpu.VMEM((3,) + tile, BF16),
            pltpu.VMEM((nx, 2 * LANES, quarter), F32),
            pltpu.VMEM((nx, 2 * LANES, middle), F32),
            pltpu.VMEM((nx, 2 * LANES, quarter), BF16),
            pltpu.VMEM((nx, 2 * LANES, quarter), BF16),
            pltpu.VMEM((nx, 2 * LANES, middle), BF16),
            pltpu.VMEM((nx, 2 * LANES, middle), BF16),
            pltpu.VMEM((nx - 1, 2 * LANES, quarter), BF16),
            pltpu.VMEM((nx - 1, 2 * LANES, quarter), BF16),
            pltpu.VMEM((nx - 1, 2 * LANES, middle), BF16),
            pltpu.VMEM((nx - 1, 2 * LANES, middle), BF16),
            pltpu.VMEM((LANES, quarter), BF16),
            pltpu.VMEM((LANES, quarter), BF16),
            pltpu.VMEM((LANES, middle), BF16),
            pltpu.VMEM((LANES, middle), BF16),
            pltpu.VMEM(tile, BF16),
            pltpu.VMEM(tile, F32),
            pltpu.SemaphoreType.DMA((4,)),
            pltpu.SemaphoreType.DMA((4,)),
            pltpu.SemaphoreType.DMA,
            pltpu.SemaphoreType.DMA((2, hop)),
            pltpu.SemaphoreType.DMA((2, 2, ny // 2, hop)),
            pltpu.SemaphoreType.DMA((2 * nx,)),
            pltpu.SemaphoreType.DMA((2 * nx,)),
            pltpu.SemaphoreType.DMA((2 * nx,)),
            pltpu.SemaphoreType.DMA((2 * nx,)),
            pltpu.SemaphoreType.DMA((8,)),
            pltpu.SemaphoreType.DMA((8,)),
            pltpu.SemaphoreType.DMA((nx,)),
            pltpu.SemaphoreType.DMA((nx,)),
            pltpu.SemaphoreType.DMA((nx,)),
            pltpu.SemaphoreType.DMA((nx,)),
            pltpu.SemaphoreType.REGULAR,
        ],
        compiler_params=pltpu.CompilerParams(
            collective_id=0, has_side_effects=True, vmem_limit_bytes=VMEM_LIMIT
        ),
    )(
        skip_gain,
        signal,
        gates,
        filters,
        out_proj.T,
        cotangent,
        first,
        twist,
        second,
        back,
        last,
    )
    return tuple(results[n] for n in range(4))


def solution(mesh):
    side = math.isqrt(mesh.shape["seq"])
    nx = mesh.shape["chan"] // CORES
    in_specs = (
        P("seq", "chan"),
        P("seq", "chan"),
        P("seq", "chan"),
        P("chan"),
        P("chan", "seq"),
        P("seq", "chan"),
    )
    out_specs = (P("seq", "chan"),) * 4
    return jax.shard_map(
        functools.partial(local, side, side, nx),
        mesh=mesh,
        in_specs=in_specs,
        out_specs=out_specs,
        check_vma=False,
    )
```

```python
import functools
import math

import jax
import jax.numpy as jnp
import ml_dtypes
import numpy as np
from jax import lax
from jax.experimental import pallas as pl
from jax.experimental.pallas import tpu as pltpu
from jax.sharding import PartitionSpec as P

LANES = 128
GROUP = 8
CORES = 2
MESH = pl.DeviceIdType.MESH
VMEM_LIMIT = 60 * 1024 * 1024
F32 = jnp.float32
BF16 = jnp.bfloat16


def halves(table):
    high = table.astype(ml_dtypes.bfloat16)
    low = (table - high.astype(np.float64)).astype(ml_dtypes.bfloat16)
    return high, low


def make_tables(blocks):
    total = 2 * blocks * LANES
    rows = -(-(blocks + 1) // 8) * 8
    k = np.arange(rows)
    j = np.arange(blocks)
    b = np.arange(LANES)
    live = (k <= blocks)[:, None].astype(np.float64)
    outer = 2 * np.pi * ((k[:, None] * j[None, :]) % (2 * blocks)) / (2 * blocks)
    first = np.concatenate([live * np.cos(outer), -live * np.sin(outer)], axis=0)
    twist = 2 * np.pi * k[:, None] * b[None, :] / total
    inner = 2 * np.pi * ((b[:, None] * b[None, :]) % LANES) / LANES
    cos, sin = np.cos(inner), np.sin(inner)
    second = np.block([[cos, -sin], [sin, cos]])
    weight = np.where((k == 0) | (k == blocks), 1.0, 2.0)[:, None] * live / total
    last = np.concatenate([weight * np.cos(outer), -weight * np.sin(outer)], axis=0).T
    return (
        np.concatenate(halves(first), axis=1),
        np.stack([np.cos(twist), -np.sin(twist)]).astype(np.float32),
        np.stack(halves(second)),
        np.stack(halves(second.T)),
        np.stack(halves(last)),
    )


def split(value):
    high = value.astype(BF16)
    return high, (value - high.astype(F32)).astype(BF16)


def mm(left, right):
    return jnp.dot(left, right, preferred_element_type=F32)


def forward(x, first, twist, second):
    rows = twist.shape[1]
    mid = mm(first[...], jnp.concatenate([x, x], axis=0))
    cos, sin = twist[0], twist[1]
    pieces = []
    for c in range(GROUP):
        re = mid[:rows, c * LANES : (c + 1) * LANES]
        im = mid[rows:, c * LANES : (c + 1) * LANES]
        pieces.append(jnp.concatenate([re * cos - im * sin, re * sin + im * cos], axis=1))
    high, low = split(jnp.concatenate(pieces, axis=0))
    return mm(high, second[0]) + mm(low, second[0]) + mm(high, second[1])


def inverse(spec, twist, back, last):
    rows = twist.shape[1]
    high, low = split(spec)
    mid = mm(high, back[0]) + mm(low, back[0]) + mm(high, back[1])
    cos, sin = twist[0], twist[1]
    pieces = []
    for c in range(GROUP):
        re = mid[c * rows : (c + 1) * rows, :LANES]
        im = mid[c * rows : (c + 1) * rows, LANES:]
        pieces.append(jnp.concatenate([re * cos + im * sin, im * cos - re * sin], axis=0))
    high, low = split(jnp.concatenate(pieces, axis=1))
    return mm(last[0], high) + mm(last[1], high) + mm(last[0], low)


def times(a, b):
    ar, ai, br, bi = a[:, :LANES], a[:, LANES:], b[:, :LANES], b[:, LANES:]
    return jnp.concatenate([ar * br - ai * bi, ar * bi + ai * br], axis=1)


def times_conj(a, b):
    ar, ai, br, bi = a[:, :LANES], a[:, LANES:], b[:, :LANES], b[:, LANES:]
    return jnp.concatenate([ar * br + ai * bi, ar * bi - ai * br], axis=1)


def kernel(
    ny,
    nz,
    nx,
    skip,
    sig_hbm,
    gat_hbm,
    fil_hbm,
    wgt_hbm,
    cot_hbm,
    first_hbm,
    twist_hbm,
    second_hbm,
    back_hbm,
    last_hbm,
    outs,
    sig,
    gat,
    fil,
    first,
    twist,
    second,
    back,
    last,
    load_sem,
    out16,
    in16,
    out8,
    in8,
    gout8,
    gin8,
    rout16,
    rin16,
    rows32,
    sf_spec,
    wt,
    order,
    cot_own,
    cot_perm,
    ck0,
    ck1,
    gp_out,
    gp_in,
    gated,
    own0,
    own1,
    ex0_out,
    ex0_in,
    ex1_out,
    ex1_in,
    mx0_out,
    mx0_in,
    mx1_out,
    mx1_in,
    ret0_out,
    ret0_in,
    ret1_out,
    ret1_in,
    perm,
    gating,
    a2a_send,
    a2a_recv,
    w_send,
    w_first,
    w_ring,
    k0_send,
    k0_recv,
    k1_send,
    k1_recv,
    p_send,
    p_recv,
    m0_send,
    m0_recv,
    m1_send,
    m1_recv,
    all_in,
):
    nseq = ny * nz
    chans = GROUP * nseq
    s = lax.axis_index("seq")
    c = lax.axis_index("chan")
    y, z = s // nz, s % nz
    x, core = c // CORES, c % CORES
    sibling = x * CORES + (1 - core)
    block = wgt_hbm.shape[0]
    half = block // 2
    quarter = chans // 4
    middle = chans // 2
    pz, py = z % 2, y % 2
    z_pair = y * nz + (z + 1 - 2 * pz)
    y_pair = (y + 1 - 2 * py) * nz + z
    keeps = core == py
    hop = ny // 2
    base = nseq * half // 2

    def cols0(n):
        return pl.ds(pl.multiple_of(n * quarter, quarter), quarter)

    def cols1(n):
        return pl.ds(pl.multiple_of(n * middle, middle), middle)

    def x_peer(dx):
        return ((x + dx) % nx) * CORES + core

    def w_rows(h, a, b):
        width = nz // 2 if h == 0 else nz
        start = pl.multiple_of(h * base + (a * width + b) * half, half)
        return wt.at[pl.ds(start, half)]

    def held(h, i, d):
        if h == 0:
            return w_rows(0, (y - d) % ny, (z // 2 - i) % hop)
        return w_rows(1, (y // 2 - i) % hop, (z - d) % nz)

    loads = [
        pltpu.make_async_copy(src, dst, load_sem.at[n])
        for n, (src, dst) in enumerate(
            (
                (wgt_hbm.at[pl.ds(0, half)], held(0, 0, 0)),
                (wgt_hbm.at[pl.ds(half, half)], held(1, 0, 0)),
                (cot_hbm, cot_own),
                (sig_hbm, sig),
                (fil_hbm, fil),
                (gat_hbm, gat),
                (first_hbm, first),
                (twist_hbm, twist),
                (second_hbm, second),
                (back_hbm, back),
                (last_hbm, last),
            )
        )
    ]
    for load in loads:
        load.start()

    bar = pltpu.get_barrier_semaphore()

    def row_peer(n):
        return y * nz + (z + n) % nz

    def column_peer(n):
        return ((y + n) % ny) * nz + z

    def greet(n, carry):
        for peer in (row_peer(n), column_peer(n)):
            pl.semaphore_signal(bar, inc=1, device_id={"seq": peer}, device_id_type=MESH)
        return carry

    lax.fori_loop(1, ny, greet, 0)
    for dx in range(1, nx):
        pl.semaphore_signal(bar, inc=1, device_id={"chan": x_peer(dx)}, device_id_type=MESH)
    pl.semaphore_signal(bar, inc=1, device_id={"chan": sibling}, device_id_type=MESH)

    loads[3].wait()
    loads[4].wait()
    out16[:, :GROUP, :] = sig[...].astype(F32).T.reshape(nseq, GROUP, LANES).astype(BF16)
    out16[:, GROUP:, :] = fil[...].astype(F32).T.reshape(nseq, GROUP, LANES).astype(BF16)
    column = lax.broadcasted_iota(jnp.int32, (chans, chans), 0)
    place = lax.broadcasted_iota(jnp.int32, (chans, chans), 1)
    zz = column // block
    rest = column % block
    target = jnp.where(
        rest < half,
        (zz % 2) * quarter + (zz // 2) * half + rest,
        middle + zz * half + rest - half,
    )
    order[...] = (place == target).astype(F32).astype(BF16)
    loads[2].wait()
    cot_perm[...] = mm(cot_own[...], order[...]).astype(BF16)
    near = pl.ds(pl.multiple_of(pz * quarter, quarter), quarter)
    far = pl.ds(pl.multiple_of((1 - pz) * quarter, quarter), quarter)
    ck0[0, :, cols0(c)] = cot_perm[:, near]

    @pl.when(keeps)
    def _():
        ck1[0, :, cols1(x)] = cot_perm[:, middle:]

    pl.semaphore_wait(bar, ny + nz + nx - 2)

    def greet_all(n, carry):
        pl.semaphore_signal(
            all_in, inc=1, device_id={"seq": row_peer(n)}, device_id_type=MESH
        )
        return carry

    lax.fori_loop(1, nz, greet_all, 0)

    def send(src, dst, send_sem, recv_sem, **where):
        pltpu.make_async_remote_copy(
            src_ref=src,
            dst_ref=dst,
            send_sem=send_sem,
            recv_sem=recv_sem,
            device_id=where,
            device_id_type=MESH,
        ).start()

    def wait(ref, sem):
        pltpu.make_async_copy(ref, ref, sem).wait()

    reach = ny // 2

    def beside(h, way):
        step = 1 - 2 * way
        return column_peer(step) if h == 0 else row_peer(step)

    def pass_on(h, way, d, i):
        sign = 1 - 2 * way
        ref = held(h, i, sign * (d - 1))
        send(ref, ref, w_send, w_ring.at[h, way, d - 1, i], seq=beside(h, way))

    def exists(way, d, parity):
        return d < reach or (d == reach and parity == way)

    def weights_begin():
        def body(n, carry):
            ref = held(0, 0, 0)
            send(ref, ref, w_send, w_first.at[0, n], seq=row_peer(2 * n))
            ref = held(1, 0, 0)
            send(ref, ref, w_send, w_first.at[1, n], seq=column_peer(2 * n))
            return carry

        lax.fori_loop(1, hop, body, 0)
        for h in range(2):
            for way in range(2):
                if exists(way, 1, 0):
                    pass_on(h, way, 1, 0)

    def weights_first(i):
        for h in range(2):
            wait(held(h, i, 0), w_first.at[h, i])
            for way in range(2):
                if exists(way, 1, i % 2):
                    pass_on(h, way, 1, i)

    def weights_step(d, i):
        for h in range(2):
            for way in range(2):
                if exists(way, d, i % 2):
                    wait(held(h, i, (1 - 2 * way) * d), w_ring.at[h, way, d - 1, i])
                    if exists(way, d + 1, i % 2):
                        pass_on(h, way, d + 1, i)

    def hops(step, size):
        return min(step, size - step)

    steps = sorted(
        ((dy, dz) for dy in range(ny) for dz in range(nz) if dy or dz),
        key=lambda step: -hops(step[0], ny) - hops(step[1], nz),
    )

    def spread(src, dst, n, part=0, parts=1):
        piece = nseq // parts
        for dy, dz in steps[part * piece : (part + 1) * piece]:
            p = ((y + dy) % ny) * nz + (z + dz) % nz
            send(src.at[p], dst.at[s], a2a_send.at[n], a2a_recv.at[n], seq=p)
        if part == 0:
            dst[pl.ds(s, 1)] = src[pl.ds(s, 1)]

    def landed(dst, n):
        wait(dst.at[pl.ds(0, nseq - 1)], a2a_recv.at[n])

    def by_channel(ref, width, start):
        return jnp.concatenate(
            [ref[pl.ds(start + n, nseq, stride=width), :] for n in range(GROUP)], axis=1
        )

    def to_blocks(ref, value, width, start):
        for n in range(GROUP):
            ref[pl.ds(start + n, nseq, stride=width), :] = value[:, n * LANES : (n + 1) * LANES]

    def gain(value):
        return jnp.concatenate(
            [
                value[:, n * LANES : (n + 1) * LANES] * skip[s * GROUP + n]
                for n in range(GROUP)
            ],
            axis=1,
        )


    def to_all(ref, send_sem, recv_sem):
        send(ref, ref, send_sem.at[0], recv_sem.at[0], chan=sibling)
        for dx in range(1, nx):
            send(ref, ref, send_sem.at[dx], recv_sem.at[dx], chan=x_peer(dx))

    def cotangent_out():
        ref = ck0.at[1, :, cols0(c)]
        wait(ref, p_recv.at[0])
        to_all(ck0.at[:, :, cols0(c)], k0_send, k0_recv)

        @pl.when(keeps)
        def _():
            wait(ck1.at[1, :, cols1(x)], p_recv.at[1])
            to_all(ck1.at[:, :, cols1(x)], k1_send, k1_recv)

    def cotangent_on():
        for dx in range(1, nx):
            ref = ck0.at[:, :, cols0(x_peer(-dx))]
            wait(ref, k0_recv.at[dx])
            send(ref, ref, k0_send.at[nx - 1 + dx], k0_recv.at[nx - 1 + dx], chan=sibling)

        @pl.when(keeps)
        def _():
            for dx in range(1, nx):
                ref = ck1.at[:, :, cols1((x - dx) % nx)]
                wait(ref, k1_recv.at[dx])
                send(ref, ref, k1_send.at[nx - 1 + dx], k1_recv.at[nx - 1 + dx], chan=sibling)

    def cotangent_in():
        wait(ck0.at[:, :, cols0(sibling)], k0_recv.at[0])
        for dx in range(1, nx):
            other = ((x - dx) % nx) * CORES + (1 - core)
            wait(ck0.at[:, :, cols0(other)], k0_recv.at[nx - 1 + dx])

        @pl.when(jnp.logical_not(keeps))
        def _():
            wait(ck1.at[:, :, cols1(x)], k1_recv.at[0])
            for dx in range(1, nx):
                wait(ck1.at[:, :, cols1((x - dx) % nx)], k1_recv.at[nx - 1 + dx])

    def tokens_out(part):
        if part == 0:
            pl.semaphore_wait(all_in, nz - 1)
        spread(out16, in16, 0, part, 4)

    def transform(n):
        if n == 0:
            landed(in16, 0)
            rows32[...] = in16[...].astype(F32).reshape(nseq * 2 * GROUP, LANES)
            for load in loads[5:]:
                load.wait()
        value = by_channel(rows32, 2 * GROUP, n * GROUP)
        sf_spec[n] = forward(value.astype(BF16), first, twist, second)

    def convolve():
        value = inverse(times(sf_spec[0], sf_spec[1]), twist, back, last)
        value += gain(by_channel(rows32, 2 * GROUP, 0))
        to_blocks(rows32, value, GROUP, 0)
        out8[...] = rows32[pl.ds(0, nseq * GROUP), :].reshape(nseq, GROUP, LANES).astype(BF16)

    def before_out(part):
        spread(out8, in8, 1, part, 4)

    def gate():
        landed(in8, 1)
        gating[...] = in8[...].astype(F32).reshape(chans, LANES).T
        gated[0] = (gating[...] * gat[...].astype(F32)).astype(BF16)

    def gate_out():
        send(gated.at[0], gated.at[1], p_send.at[4], p_recv.at[4], seq=z_pair)
        send(gated.at[0], gated.at[2], p_send.at[5], p_recv.at[5], seq=y_pair)

    loads[0].wait()
    loads[1].wait()
    weights_begin()
    send(cot_perm.at[:, far], ck0.at[1, :, cols0(c)], p_send.at[0], p_recv.at[0], seq=z_pair)

    @pl.when(jnp.logical_not(keeps))
    def _():
        send(
            cot_perm.at[:, pl.ds(middle, middle)],
            ck1.at[1, :, cols1(x)],
            p_send.at[1],
            p_recv.at[1],
            seq=y_pair,
        )

    weights_first(1)
    weights_first(3)
    weights_first(2)
    cotangent_out()
    weights_step(1, 0)
    tokens_out(0)
    weights_step(1, 1)
    tokens_out(1)
    weights_step(1, 3)
    tokens_out(2)
    weights_step(1, 2)
    tokens_out(3)
    weights_step(2, 0)
    cotangent_on()
    weights_step(2, 1)
    weights_step(2, 3)
    weights_step(2, 2)
    transform(0)
    weights_step(3, 0)
    transform(1)
    weights_step(3, 1)
    convolve()
    weights_step(3, 3)
    before_out(0)
    weights_step(3, 2)
    before_out(1)
    weights_step(4, 0)
    before_out(2)
    weights_step(4, 1)
    before_out(3)
    cotangent_in()
    weights_step(4, 3)
    weights_step(4, 2)

    gp_out[0] = mm(ck0[1], wt[pl.ds(0, base), :]).astype(BF16)
    send(gp_out.at[0], gp_in.at[0], p_send.at[2], p_recv.at[2], seq=z_pair)
    gp_out[1] = mm(ck1[1], wt[pl.ds(base, base), :]).astype(BF16)
    send(gp_out.at[1], gp_in.at[1], p_send.at[3], p_recv.at[3], seq=y_pair)
    mine = mm(ck0[0], wt[pl.ds(0, base), :]) + mm(ck1[0], wt[pl.ds(base, base), :])

    gate()
    gate_out()
    wait(gp_in.at[0], p_recv.at[2])
    wait(gp_in.at[1], p_recv.at[3])
    gates = gat[...].astype(F32)
    total = mine + gp_in[0].astype(F32) + gp_in[1].astype(F32)
    gconv = (total * gates).T
    gout8[...] = gconv.reshape(nseq, GROUP, LANES).astype(BF16)
    spread(gout8, gin8, 2)
    outs[2] = (total * gating[...]).astype(BF16)

    wait(gated.at[1], p_recv.at[4])
    wait(gated.at[2], p_recv.at[5])

    def part(tokens, start, width):
        return lax.dot_general(
            tokens,
            wt[pl.ds(pl.multiple_of(start, width), width), :],
            (((1,), (1,)), ((), ())),
            preferred_element_type=F32,
        )

    z_tokens = jnp.concatenate([gated[0], gated[1]], axis=0)
    y_tokens = jnp.concatenate([gated[0], gated[2]], axis=0)

    def part0(n):
        return part(z_tokens, n * quarter, quarter)

    def part1(n):
        return part(y_tokens, base + n * middle, middle)

    for n in range(nx):
        ex0_out[n] = part0(n * CORES + (1 - core)).astype(BF16)
    send(ex0_out, ex0_in, m0_send.at[0], m0_recv.at[0], chan=sibling)

    @pl.when(jnp.logical_not(keeps))
    def _():
        for n in range(nx):
            ex1_out[n] = part1(n).astype(BF16)
        send(ex1_out, ex1_in, m1_send.at[0], m1_recv.at[0], chan=sibling)

    for n in range(nx):
        own0[n] = part0(n * CORES + core)

    @pl.when(keeps)
    def _():
        for n in range(nx):
            own1[n] = part1(n)
        wait(ex1_in, m1_recv.at[0])
        own1[...] += ex1_in[...].astype(F32)
        for dx in range(1, nx):
            mx1_out[dx - 1] = own1[(x + dx) % nx].astype(BF16)
            send(
                mx1_out.at[dx - 1],
                mx1_in.at[dx - 1],
                m1_send.at[dx],
                m1_recv.at[dx],
                chan=x_peer(dx),
            )

    wait(ex0_in, m0_recv.at[0])
    own0[...] += ex0_in[...].astype(F32)
    for dx in range(1, nx):
        mx0_out[dx - 1] = own0[(x + dx) % nx].astype(BF16)
        send(
            mx0_out.at[dx - 1],
            mx0_in.at[dx - 1],
            m0_send.at[dx],
            m0_recv.at[dx],
            chan=x_peer(dx),
        )

    landed(gin8, 2)
    rows32[pl.ds(0, nseq * GROUP), :] = gin8[...].astype(F32).reshape(nseq * GROUP, LANES)
    grad_x = by_channel(rows32, GROUP, 0)
    g_spec = forward(grad_x.astype(BF16), first, twist, second)
    through = inverse(times_conj(sf_spec[1], g_spec), twist, back, last)
    kern = inverse(times_conj(sf_spec[0], g_spec), twist, back, last)
    to_blocks(rows32, through + gain(grad_x), 2 * GROUP, 0)
    to_blocks(rows32, kern * (1.0 / math.sqrt(nseq * LANES)), 2 * GROUP, GROUP)
    rout16[...] = rows32[...].reshape(nseq, 2 * GROUP, LANES).astype(BF16)
    spread(rout16, rin16, 3)

    @pl.when(keeps)
    def _():
        result = own1[x]
        for dx in range(1, nx):
            wait(mx1_in.at[dx - 1], m1_recv.at[dx])
            result += mx1_in[dx - 1].astype(F32)
        perm[:, middle:] = result[:LANES].astype(BF16)
        ret1_out[...] = result[LANES:].astype(BF16)
        send(ret1_out, ret1_in, p_send.at[7], p_recv.at[7], seq=y_pair)

    result = own0[x]
    for dx in range(1, nx):
        wait(mx0_in.at[dx - 1], m0_recv.at[dx])
        result += mx0_in[dx - 1].astype(F32)
    perm[:, near] = result[:LANES].astype(BF16)
    ret0_out[...] = result[LANES:].astype(BF16)
    send(ret0_out, ret0_in, p_send.at[6], p_recv.at[6], seq=z_pair)

    wait(ret0_in, p_recv.at[6])
    perm[:, far] = ret0_in[...]

    @pl.when(jnp.logical_not(keeps))
    def _():
        wait(ret1_in, p_recv.at[7])
        perm[:, middle:] = ret1_in[...]

    outs[0] = lax.dot_general(
        perm[...], order[...], (((1,), (1,)), ((), ())), preferred_element_type=F32
    ).astype(BF16)

    landed(rin16, 3)
    grads = rin16[...].astype(F32)
    outs[1] = grads[:, :GROUP, :].reshape(chans, LANES).T.astype(BF16)
    outs[3] = grads[:, GROUP:, :].reshape(chans, LANES).T.astype(BF16)

    for n, src in enumerate((out16, out8, gout8, rout16)):
        wait(src.at[pl.ds(0, nseq - 1)], a2a_send.at[n])
    wait(wt.at[pl.ds(0, (2 * (hop - 1) + 2 * hop * (2 * reach - 1)) * half)], w_send)
    for n in range(2 * nx - 1):
        wait(ck0.at[:, :, cols0(0)], k0_send.at[n])
    wait(ck0.at[1, :, cols0(0)], p_send.at[0])
    wait(gp_out.at[0], p_send.at[2])
    wait(gp_out.at[1], p_send.at[3])
    wait(gated.at[0], p_send.at[4])
    wait(gated.at[0], p_send.at[5])
    wait(ret0_out, p_send.at[6])
    wait(ex0_out, m0_send.at[0])
    for dx in range(1, nx):
        wait(mx0_out.at[dx - 1], m0_send.at[dx])

    @pl.when(keeps)
    def _():
        for n in range(2 * nx - 1):
            wait(ck1.at[:, :, cols1(0)], k1_send.at[n])
        for dx in range(1, nx):
            wait(mx1_out.at[dx - 1], m1_send.at[dx])
        wait(ret1_out, p_send.at[7])

    @pl.when(jnp.logical_not(keeps))
    def _():
        wait(ck1.at[1, :, cols1(0)], p_send.at[1])
        wait(ex1_out, m1_send.at[0])


def local(ny, nz, nx, signal, gates, filters, skip_gain, out_proj, cotangent):
    nseq = ny * nz
    chans = signal.shape[1]
    half = out_proj.shape[1] // 2
    quarter, middle = chans // 4, chans // 2
    hop = ny // 2
    first, twist, second, back, last = make_tables(nseq)
    rows = twist.shape[1]
    hbm = pl.BlockSpec(memory_space=pltpu.HBM)
    vmem = pl.BlockSpec(memory_space=pltpu.VMEM)
    smem = pl.BlockSpec(memory_space=pltpu.SMEM)
    out = jax.ShapeDtypeStruct((LANES, chans), BF16)
    wide = (nseq, 2 * GROUP, LANES)
    narrow = (nseq, GROUP, LANES)
    tile = (LANES, chans)
    results = pl.pallas_call(
        functools.partial(kernel, ny, nz, nx),
        out_shape=jax.ShapeDtypeStruct((4, LANES, chans), BF16),
        in_specs=[smem] + [hbm] * 10,
        out_specs=vmem,
        scratch_shapes=[
            pltpu.VMEM(tile, BF16),
            pltpu.VMEM(tile, BF16),
            pltpu.VMEM(tile, BF16),
            pltpu.VMEM(first.shape, BF16),
            pltpu.VMEM(twist.shape, F32),
            pltpu.VMEM(second.shape, BF16),
            pltpu.VMEM(back.shape, BF16),
            pltpu.VMEM(last.shape, BF16),
            pltpu.SemaphoreType.DMA((11,)),
            pltpu.VMEM(wide, BF16),
            pltpu.VMEM(wide, BF16),
            pltpu.VMEM(narrow, BF16),
            pltpu.VMEM(narrow, BF16),
            pltpu.VMEM(narrow, BF16),
            pltpu.VMEM(narrow, BF16),
            pltpu.VMEM(wide, BF16),
            pltpu.VMEM(wide, BF16),
            pltpu.VMEM((nseq * 2 * GROUP, LANES), F32),
            pltpu.VMEM((2, GROUP * rows, 2 * LANES), F32),
            pltpu.VMEM((nseq * half, chans), BF16),
            pltpu.VMEM((chans, chans), BF16),
            pltpu.VMEM(tile, BF16),
            pltpu.VMEM(tile, BF16),
            pltpu.VMEM((2, LANES, nx * CORES * quarter), BF16),
            pltpu.VMEM((2, LANES, nx * middle), BF16),
            pltpu.VMEM((2,) + tile, BF16),
            pltpu.VMEM((2,) + tile, BF16),
            pltpu.VMEM((3,) + tile, BF16),
            pltpu.VMEM((nx, 2 * LANES, quarter), F32),
            pltpu.VMEM((nx, 2 * LANES, middle), F32),
            pltpu.VMEM((nx, 2 * LANES, quarter), BF16),
            pltpu.VMEM((nx, 2 * LANES, quarter), BF16),
            pltpu.VMEM((nx, 2 * LANES, middle), BF16),
            pltpu.VMEM((nx, 2 * LANES, middle), BF16),
            pltpu.VMEM((nx - 1, 2 * LANES, quarter), BF16),
            pltpu.VMEM((nx - 1, 2 * LANES, quarter), BF16),
            pltpu.VMEM((nx - 1, 2 * LANES, middle), BF16),
            pltpu.VMEM((nx - 1, 2 * LANES, middle), BF16),
            pltpu.VMEM((LANES, quarter), BF16),
            pltpu.VMEM((LANES, quarter), BF16),
            pltpu.VMEM((LANES, middle), BF16),
            pltpu.VMEM((LANES, middle), BF16),
            pltpu.VMEM(tile, BF16),
            pltpu.VMEM(tile, F32),
            pltpu.SemaphoreType.DMA((4,)),
            pltpu.SemaphoreType.DMA((4,)),
            pltpu.SemaphoreType.DMA,
            pltpu.SemaphoreType.DMA((2, hop)),
            pltpu.SemaphoreType.DMA((2, 2, ny // 2, hop)),
            pltpu.SemaphoreType.DMA((2 * nx,)),
            pltpu.SemaphoreType.DMA((2 * nx,)),
            pltpu.SemaphoreType.DMA((2 * nx,)),
            pltpu.SemaphoreType.DMA((2 * nx,)),
            pltpu.SemaphoreType.DMA((8,)),
            pltpu.SemaphoreType.DMA((8,)),
            pltpu.SemaphoreType.DMA((nx,)),
            pltpu.SemaphoreType.DMA((nx,)),
            pltpu.SemaphoreType.DMA((nx,)),
            pltpu.SemaphoreType.DMA((nx,)),
            pltpu.SemaphoreType.REGULAR,
        ],
        compiler_params=pltpu.CompilerParams(
            collective_id=0, has_side_effects=True, vmem_limit_bytes=VMEM_LIMIT
        ),
    )(
        skip_gain,
        signal,
        gates,
        filters,
        out_proj.T,
        cotangent,
        first,
        twist,
        second,
        back,
        last,
    )
    return tuple(results[n] for n in range(4))


def solution(mesh):
    side = math.isqrt(mesh.shape["seq"])
    nx = mesh.shape["chan"] // CORES
    in_specs = (
        P("seq", "chan"),
        P("seq", "chan"),
        P("seq", "chan"),
        P("chan"),
        P("chan", "seq"),
        P("seq", "chan"),
    )
    out_specs = (P("seq", "chan"),) * 4
    return jax.shard_map(
        functools.partial(local, side, side, nx),
        mesh=mesh,
        in_specs=in_specs,
        out_specs=out_specs,
        check_vma=False,
    )
```

```python
import functools
import math

import jax
import jax.numpy as jnp
import ml_dtypes
import numpy as np
from jax import lax
from jax.experimental import pallas as pl
from jax.experimental.pallas import tpu as pltpu
from jax.sharding import PartitionSpec as P

LANES = 128
GROUP = 8
CORES = 2
MESH = pl.DeviceIdType.MESH
VMEM_LIMIT = 60 * 1024 * 1024
F32 = jnp.float32
BF16 = jnp.bfloat16


def halves(table):
    high = table.astype(ml_dtypes.bfloat16)
    low = (table - high.astype(np.float64)).astype(ml_dtypes.bfloat16)
    return high, low


def make_tables(blocks):
    total = 2 * blocks * LANES
    rows = -(-(blocks + 1) // 8) * 8
    k = np.arange(rows)
    j = np.arange(blocks)
    b = np.arange(LANES)
    live = (k <= blocks)[:, None].astype(np.float64)
    outer = 2 * np.pi * ((k[:, None] * j[None, :]) % (2 * blocks)) / (2 * blocks)
    first = np.concatenate([live * np.cos(outer), -live * np.sin(outer)], axis=0)
    twist = 2 * np.pi * k[:, None] * b[None, :] / total
    inner = 2 * np.pi * ((b[:, None] * b[None, :]) % LANES) / LANES
    cos, sin = np.cos(inner), np.sin(inner)
    second = np.block([[cos, -sin], [sin, cos]])
    weight = np.where((k == 0) | (k == blocks), 1.0, 2.0)[:, None] * live / total
    last = np.concatenate([weight * np.cos(outer), -weight * np.sin(outer)], axis=0).T
    return (
        np.concatenate(halves(first), axis=1),
        np.stack([np.cos(twist), -np.sin(twist)]).astype(np.float32),
        np.stack(halves(second)),
        np.stack(halves(second.T)),
        np.stack(halves(last)),
    )


def split(value):
    high = value.astype(BF16)
    return high, (value - high.astype(F32)).astype(BF16)


def mm(left, right):
    return jnp.dot(left, right, preferred_element_type=F32)


def forward(x, first, twist, second):
    rows = twist.shape[1]
    mid = mm(first[...], jnp.concatenate([x, x], axis=0))
    cos, sin = twist[0], twist[1]
    pieces = []
    for c in range(GROUP):
        re = mid[:rows, c * LANES : (c + 1) * LANES]
        im = mid[rows:, c * LANES : (c + 1) * LANES]
        pieces.append(jnp.concatenate([re * cos - im * sin, re * sin + im * cos], axis=1))
    high, low = split(jnp.concatenate(pieces, axis=0))
    return mm(high, second[0]) + mm(low, second[0]) + mm(high, second[1])


def inverse(spec, twist, back, last):
    rows = twist.shape[1]
    high, low = split(spec)
    mid = mm(high, back[0]) + mm(low, back[0]) + mm(high, back[1])
    cos, sin = twist[0], twist[1]
    pieces = []
    for c in range(spec.shape[0] // rows):
        re = mid[c * rows : (c + 1) * rows, :LANES]
        im = mid[c * rows : (c + 1) * rows, LANES:]
        pieces.append(jnp.concatenate([re * cos + im * sin, im * cos - re * sin], axis=0))
    high, low = split(jnp.concatenate(pieces, axis=1))
    return mm(last[0], high) + mm(last[1], high) + mm(last[0], low)


def times(a, b):
    ar, ai, br, bi = a[:, :LANES], a[:, LANES:], b[:, :LANES], b[:, LANES:]
    return jnp.concatenate([ar * br - ai * bi, ar * bi + ai * br], axis=1)


def times_conj(a, b):
    ar, ai, br, bi = a[:, :LANES], a[:, LANES:], b[:, :LANES], b[:, LANES:]
    return jnp.concatenate([ar * br + ai * bi, ar * bi - ai * br], axis=1)


def kernel(
    ny,
    nz,
    nx,
    skip,
    sig_hbm,
    gat_hbm,
    fil_hbm,
    wgt_hbm,
    cot_hbm,
    first_hbm,
    twist_hbm,
    second_hbm,
    back_hbm,
    last_hbm,
    outs,
    sig,
    gat,
    fil,
    first,
    twist,
    second,
    back,
    last,
    load_sem,
    out16,
    in16,
    out8,
    in8,
    gout8,
    gin8,
    rout16,
    rin16,
    rows32,
    sf_spec,
    wt,
    order,
    cot_own,
    cot_perm,
    ck0,
    ck1,
    gp_out,
    gp_in,
    gated,
    own0,
    own1,
    ex0_out,
    ex0_in,
    ex1_out,
    ex1_in,
    mx0_out,
    mx0_in,
    mx1_out,
    mx1_in,
    ret0_out,
    ret0_in,
    ret1_out,
    ret1_in,
    perm,
    gating,
    a2a_send,
    a2a_recv,
    w_send,
    w_first,
    w_ring,
    k0_send,
    k0_recv,
    k1_send,
    k1_recv,
    p_send,
    p_recv,
    m0_send,
    m0_recv,
    m1_send,
    m1_recv,
    all_in,
):
    nseq = ny * nz
    chans = GROUP * nseq
    s = lax.axis_index("seq")
    c = lax.axis_index("chan")
    y, z = s // nz, s % nz
    x, core = c // CORES, c % CORES
    sibling = x * CORES + (1 - core)
    block = wgt_hbm.shape[0]
    half = block // 2
    quarter = chans // 4
    middle = chans // 2
    pz, py = z % 2, y % 2
    z_pair = y * nz + (z + 1 - 2 * pz)
    y_pair = (y + 1 - 2 * py) * nz + z
    keeps = core == py
    hop = ny // 2
    base = nseq * half // 2

    def cols0(n):
        return pl.ds(pl.multiple_of(n * quarter, quarter), quarter)

    def cols1(n):
        return pl.ds(pl.multiple_of(n * middle, middle), middle)

    def x_peer(dx):
        return ((x + dx) % nx) * CORES + core

    def w_rows(h, a, b):
        width = nz // 2 if h == 0 else nz
        start = pl.multiple_of(h * base + (a * width + b) * half, half)
        return wt.at[pl.ds(start, half)]

    def held(h, i, d):
        if h == 0:
            return w_rows(0, (y - d) % ny, (z // 2 - i) % hop)
        return w_rows(1, (y // 2 - i) % hop, (z - d) % nz)

    loads = [
        pltpu.make_async_copy(src, dst, load_sem.at[n])
        for n, (src, dst) in enumerate(
            (
                (wgt_hbm.at[pl.ds(0, half)], held(0, 0, 0)),
                (wgt_hbm.at[pl.ds(half, half)], held(1, 0, 0)),
                (cot_hbm, cot_own),
                (sig_hbm, sig),
                (fil_hbm, fil),
                (gat_hbm, gat),
                (first_hbm, first),
                (twist_hbm, twist),
                (second_hbm, second),
                (back_hbm, back),
                (last_hbm, last),
            )
        )
    ]
    for load in loads:
        load.start()

    bar = pltpu.get_barrier_semaphore()

    def row_peer(n):
        return y * nz + (z + n) % nz

    def column_peer(n):
        return ((y + n) % ny) * nz + z

    def greet(n, carry):
        for peer in (row_peer(n), column_peer(n)):
            pl.semaphore_signal(bar, inc=1, device_id={"seq": peer}, device_id_type=MESH)
        return carry

    lax.fori_loop(1, ny, greet, 0)
    for dx in range(1, nx):
        pl.semaphore_signal(bar, inc=1, device_id={"chan": x_peer(dx)}, device_id_type=MESH)
    pl.semaphore_signal(bar, inc=1, device_id={"chan": sibling}, device_id_type=MESH)

    loads[3].wait()
    loads[4].wait()
    out16[:, :GROUP, :] = sig[...].astype(F32).T.reshape(nseq, GROUP, LANES).astype(BF16)
    out16[:, GROUP:, :] = fil[...].astype(F32).T.reshape(nseq, GROUP, LANES).astype(BF16)
    column = lax.broadcasted_iota(jnp.int32, (chans, chans), 0)
    place = lax.broadcasted_iota(jnp.int32, (chans, chans), 1)
    zz = column // block
    rest = column % block
    target = jnp.where(
        rest < half,
        (zz % 2) * quarter + (zz // 2) * half + rest,
        middle + zz * half + rest - half,
    )
    order[...] = (place == target).astype(F32).astype(BF16)
    loads[2].wait()
    cot_perm[...] = mm(cot_own[...], order[...]).astype(BF16)
    near = pl.ds(pl.multiple_of(pz * quarter, quarter), quarter)
    far = pl.ds(pl.multiple_of((1 - pz) * quarter, quarter), quarter)
    ck0[0, :, cols0(c)] = cot_perm[:, near]

    @pl.when(keeps)
    def _():
        ck1[0, :, cols1(x)] = cot_perm[:, middle:]

    pl.semaphore_wait(bar, ny + nz + nx - 2)

    def greet_all(n, carry):
        pl.semaphore_signal(
            all_in, inc=1, device_id={"seq": row_peer(n)}, device_id_type=MESH
        )
        return carry

    lax.fori_loop(1, nz, greet_all, 0)

    def send(src, dst, send_sem, recv_sem, **where):
        pltpu.make_async_remote_copy(
            src_ref=src,
            dst_ref=dst,
            send_sem=send_sem,
            recv_sem=recv_sem,
            device_id=where,
            device_id_type=MESH,
        ).start()

    def wait(ref, sem):
        pltpu.make_async_copy(ref, ref, sem).wait()

    reach = ny // 2

    def beside(h, way):
        step = 1 - 2 * way
        return column_peer(step) if h == 0 else row_peer(step)

    def pass_on(h, way, d, i):
        sign = 1 - 2 * way
        ref = held(h, i, sign * (d - 1))
        send(ref, ref, w_send, w_ring.at[h, way, d - 1, i], seq=beside(h, way))

    def exists(way, d, parity):
        return d < reach or (d == reach and parity == way)

    def weights_begin():
        def body(n, carry):
            ref = held(0, 0, 0)
            send(ref, ref, w_send, w_first.at[0, n], seq=row_peer(2 * n))
            ref = held(1, 0, 0)
            send(ref, ref, w_send, w_first.at[1, n], seq=column_peer(2 * n))
            return carry

        lax.fori_loop(1, hop, body, 0)
        for h in range(2):
            for way in range(2):
                if exists(way, 1, 0):
                    pass_on(h, way, 1, 0)

    def weights_first(i):
        for h in range(2):
            wait(held(h, i, 0), w_first.at[h, i])
            for way in range(2):
                if exists(way, 1, i % 2):
                    pass_on(h, way, 1, i)

    def weights_step(d, i):
        for h in range(2):
            for way in range(2):
                if exists(way, d, i % 2):
                    wait(held(h, i, (1 - 2 * way) * d), w_ring.at[h, way, d - 1, i])
                    if exists(way, d + 1, i % 2):
                        pass_on(h, way, d + 1, i)

    def hops(step, size):
        return min(step, size - step)

    steps = sorted(
        ((dy, dz) for dy in range(ny) for dz in range(nz) if dy or dz),
        key=lambda step: -hops(step[0], ny) - hops(step[1], nz),
    )

    def spread(src, dst, n, part=0, parts=1):
        piece = nseq // parts
        for dy, dz in steps[part * piece : (part + 1) * piece]:
            p = ((y + dy) % ny) * nz + (z + dz) % nz
            send(src.at[p], dst.at[s], a2a_send.at[n], a2a_recv.at[n], seq=p)
        if part == 0:
            dst[pl.ds(s, 1)] = src[pl.ds(s, 1)]

    def landed(dst, n):
        wait(dst.at[pl.ds(0, nseq - 1)], a2a_recv.at[n])

    def by_channel(ref, width, start):
        return jnp.concatenate(
            [ref[pl.ds(start + n, nseq, stride=width), :] for n in range(GROUP)], axis=1
        )

    def to_blocks(ref, value, width, start):
        for n in range(GROUP):
            ref[pl.ds(start + n, nseq, stride=width), :] = value[:, n * LANES : (n + 1) * LANES]

    def gain(value):
        return jnp.concatenate(
            [
                value[:, n * LANES : (n + 1) * LANES] * skip[s * GROUP + n]
                for n in range(GROUP)
            ],
            axis=1,
        )


    def to_all(ref, send_sem, recv_sem):
        send(ref, ref, send_sem.at[0], recv_sem.at[0], chan=sibling)
        for dx in range(1, nx):
            send(ref, ref, send_sem.at[dx], recv_sem.at[dx], chan=x_peer(dx))

    def cotangent_out():
        ref = ck0.at[1, :, cols0(c)]
        wait(ref, p_recv.at[0])
        to_all(ck0.at[:, :, cols0(c)], k0_send, k0_recv)

        @pl.when(keeps)
        def _():
            wait(ck1.at[1, :, cols1(x)], p_recv.at[1])
            to_all(ck1.at[:, :, cols1(x)], k1_send, k1_recv)

    def cotangent_on():
        for dx in range(1, nx):
            ref = ck0.at[:, :, cols0(x_peer(-dx))]
            wait(ref, k0_recv.at[dx])
            send(ref, ref, k0_send.at[nx - 1 + dx], k0_recv.at[nx - 1 + dx], chan=sibling)

        @pl.when(keeps)
        def _():
            for dx in range(1, nx):
                ref = ck1.at[:, :, cols1((x - dx) % nx)]
                wait(ref, k1_recv.at[dx])
                send(ref, ref, k1_send.at[nx - 1 + dx], k1_recv.at[nx - 1 + dx], chan=sibling)

    def cotangent_in():
        wait(ck0.at[:, :, cols0(sibling)], k0_recv.at[0])
        for dx in range(1, nx):
            other = ((x - dx) % nx) * CORES + (1 - core)
            wait(ck0.at[:, :, cols0(other)], k0_recv.at[nx - 1 + dx])

        @pl.when(jnp.logical_not(keeps))
        def _():
            wait(ck1.at[:, :, cols1(x)], k1_recv.at[0])
            for dx in range(1, nx):
                wait(ck1.at[:, :, cols1((x - dx) % nx)], k1_recv.at[nx - 1 + dx])

    def tokens_out(part):
        if part == 0:
            pl.semaphore_wait(all_in, nz - 1)
        spread(out16, in16, 0, part, 4)

    def transform(n):
        if n == 0:
            landed(in16, 0)
            rows32[...] = in16[...].astype(F32).reshape(nseq * 2 * GROUP, LANES)
            for load in loads[5:]:
                load.wait()
        value = by_channel(rows32, 2 * GROUP, n * GROUP)
        sf_spec[n] = forward(value.astype(BF16), first, twist, second)

    def convolve():
        value = inverse(times(sf_spec[0], sf_spec[1]), twist, back, last)
        value += gain(by_channel(rows32, 2 * GROUP, 0))
        to_blocks(rows32, value, GROUP, 0)
        out8[...] = rows32[pl.ds(0, nseq * GROUP), :].reshape(nseq, GROUP, LANES).astype(BF16)

    def before_out(part):
        spread(out8, in8, 1, part, 4)

    def gate():
        landed(in8, 1)
        gating[...] = in8[...].astype(F32).reshape(chans, LANES).T
        gated[0] = (gating[...] * gat[...].astype(F32)).astype(BF16)

    def gate_out():
        send(gated.at[0], gated.at[1], p_send.at[4], p_recv.at[4], seq=z_pair)
        send(gated.at[0], gated.at[2], p_send.at[5], p_recv.at[5], seq=y_pair)

    loads[0].wait()
    loads[1].wait()
    weights_begin()
    send(cot_perm.at[:, far], ck0.at[1, :, cols0(c)], p_send.at[0], p_recv.at[0], seq=z_pair)

    @pl.when(jnp.logical_not(keeps))
    def _():
        send(
            cot_perm.at[:, pl.ds(middle, middle)],
            ck1.at[1, :, cols1(x)],
            p_send.at[1],
            p_recv.at[1],
            seq=y_pair,
        )

    weights_first(1)
    weights_first(3)
    weights_first(2)
    cotangent_out()
    weights_step(1, 0)
    tokens_out(0)
    weights_step(1, 1)
    tokens_out(1)
    weights_step(1, 3)
    tokens_out(2)
    weights_step(1, 2)
    tokens_out(3)
    weights_step(2, 0)
    cotangent_on()
    weights_step(2, 1)
    weights_step(2, 3)
    weights_step(2, 2)
    transform(0)
    weights_step(3, 0)
    transform(1)
    weights_step(3, 1)
    convolve()
    weights_step(3, 3)
    before_out(0)
    weights_step(3, 2)
    before_out(1)
    weights_step(4, 0)
    before_out(2)
    weights_step(4, 1)
    before_out(3)
    cotangent_in()
    weights_step(4, 3)
    weights_step(4, 2)

    gp_out[0] = mm(ck0[1], wt[pl.ds(0, base), :]).astype(BF16)
    send(gp_out.at[0], gp_in.at[0], p_send.at[2], p_recv.at[2], seq=z_pair)
    gp_out[1] = mm(ck1[1], wt[pl.ds(base, base), :]).astype(BF16)
    send(gp_out.at[1], gp_in.at[1], p_send.at[3], p_recv.at[3], seq=y_pair)
    mine = mm(ck0[0], wt[pl.ds(0, base), :]) + mm(ck1[0], wt[pl.ds(base, base), :])

    gate()
    gate_out()
    wait(gp_in.at[0], p_recv.at[2])
    wait(gp_in.at[1], p_recv.at[3])
    gates = gat[...].astype(F32)
    total = mine + gp_in[0].astype(F32) + gp_in[1].astype(F32)
    gconv = (total * gates).T
    gout8[...] = gconv.reshape(nseq, GROUP, LANES).astype(BF16)
    spread(gout8, gin8, 2)
    outs[2] = (total * gating[...]).astype(BF16)

    wait(gated.at[1], p_recv.at[4])
    wait(gated.at[2], p_recv.at[5])

    def part(tokens, start, width):
        return lax.dot_general(
            tokens,
            wt[pl.ds(pl.multiple_of(start, width), width), :],
            (((1,), (1,)), ((), ())),
            preferred_element_type=F32,
        )

    z_tokens = jnp.concatenate([gated[0], gated[1]], axis=0)
    y_tokens = jnp.concatenate([gated[0], gated[2]], axis=0)

    def part0(n):
        return part(z_tokens, n * quarter, quarter)

    def part1(n):
        return part(y_tokens, base + n * middle, middle)

    for n in range(nx):
        ex0_out[n] = part0(n * CORES + (1 - core)).astype(BF16)
    send(ex0_out, ex0_in, m0_send.at[0], m0_recv.at[0], chan=sibling)

    @pl.when(jnp.logical_not(keeps))
    def _():
        for n in range(nx):
            ex1_out[n] = part1(n).astype(BF16)
        send(ex1_out, ex1_in, m1_send.at[0], m1_recv.at[0], chan=sibling)

    for n in range(nx):
        own0[n] = part0(n * CORES + core)

    @pl.when(keeps)
    def _():
        for n in range(nx):
            own1[n] = part1(n)
        wait(ex1_in, m1_recv.at[0])
        own1[...] += ex1_in[...].astype(F32)
        for dx in range(1, nx):
            mx1_out[dx - 1] = own1[(x + dx) % nx].astype(BF16)
            send(
                mx1_out.at[dx - 1],
                mx1_in.at[dx - 1],
                m1_send.at[dx],
                m1_recv.at[dx],
                chan=x_peer(dx),
            )

    wait(ex0_in, m0_recv.at[0])
    own0[...] += ex0_in[...].astype(F32)
    for dx in range(1, nx):
        mx0_out[dx - 1] = own0[(x + dx) % nx].astype(BF16)
        send(
            mx0_out.at[dx - 1],
            mx0_in.at[dx - 1],
            m0_send.at[dx],
            m0_recv.at[dx],
            chan=x_peer(dx),
        )

    landed(gin8, 2)
    rows32[pl.ds(0, nseq * GROUP), :] = gin8[...].astype(F32).reshape(nseq * GROUP, LANES)
    grad_x = by_channel(rows32, GROUP, 0)
    g_spec = forward(grad_x.astype(BF16), first, twist, second)
    products = [times_conj(sf_spec[1], g_spec), times_conj(sf_spec[0], g_spec)]
    both = inverse(jnp.concatenate(products, axis=0), twist, back, last)
    through, kern = both[:, : GROUP * LANES], both[:, GROUP * LANES :]
    to_blocks(rows32, through + gain(grad_x), 2 * GROUP, 0)
    to_blocks(rows32, kern * (1.0 / math.sqrt(nseq * LANES)), 2 * GROUP, GROUP)
    rout16[...] = rows32[...].reshape(nseq, 2 * GROUP, LANES).astype(BF16)
    spread(rout16, rin16, 3)

    @pl.when(keeps)
    def _():
        result = own1[x]
        for dx in range(1, nx):
            wait(mx1_in.at[dx - 1], m1_recv.at[dx])
            result += mx1_in[dx - 1].astype(F32)
        perm[:, middle:] = result[:LANES].astype(BF16)
        ret1_out[...] = result[LANES:].astype(BF16)
        send(ret1_out, ret1_in, p_send.at[7], p_recv.at[7], seq=y_pair)

    result = own0[x]
    for dx in range(1, nx):
        wait(mx0_in.at[dx - 1], m0_recv.at[dx])
        result += mx0_in[dx - 1].astype(F32)
    perm[:, near] = result[:LANES].astype(BF16)
    ret0_out[...] = result[LANES:].astype(BF16)
    send(ret0_out, ret0_in, p_send.at[6], p_recv.at[6], seq=z_pair)

    wait(ret0_in, p_recv.at[6])
    perm[:, far] = ret0_in[...]

    @pl.when(jnp.logical_not(keeps))
    def _():
        wait(ret1_in, p_recv.at[7])
        perm[:, middle:] = ret1_in[...]

    outs[0] = lax.dot_general(
        perm[...], order[...], (((1,), (1,)), ((), ())), preferred_element_type=F32
    ).astype(BF16)

    landed(rin16, 3)
    grads = rin16[...].astype(F32)
    outs[1] = grads[:, :GROUP, :].reshape(chans, LANES).T.astype(BF16)
    outs[3] = grads[:, GROUP:, :].reshape(chans, LANES).T.astype(BF16)

    for n, src in enumerate((out16, out8, gout8, rout16)):
        wait(src.at[pl.ds(0, nseq - 1)], a2a_send.at[n])
    wait(wt.at[pl.ds(0, (2 * (hop - 1) + 2 * hop * (2 * reach - 1)) * half)], w_send)
    for n in range(2 * nx - 1):
        wait(ck0.at[:, :, cols0(0)], k0_send.at[n])
    wait(ck0.at[1, :, cols0(0)], p_send.at[0])
    wait(gp_out.at[0], p_send.at[2])
    wait(gp_out.at[1], p_send.at[3])
    wait(gated.at[0], p_send.at[4])
    wait(gated.at[0], p_send.at[5])
    wait(ret0_out, p_send.at[6])
    wait(ex0_out, m0_send.at[0])
    for dx in range(1, nx):
        wait(mx0_out.at[dx - 1], m0_send.at[dx])

    @pl.when(keeps)
    def _():
        for n in range(2 * nx - 1):
            wait(ck1.at[:, :, cols1(0)], k1_send.at[n])
        for dx in range(1, nx):
            wait(mx1_out.at[dx - 1], m1_send.at[dx])
        wait(ret1_out, p_send.at[7])

    @pl.when(jnp.logical_not(keeps))
    def _():
        wait(ck1.at[1, :, cols1(0)], p_send.at[1])
        wait(ex1_out, m1_send.at[0])


def local(ny, nz, nx, signal, gates, filters, skip_gain, out_proj, cotangent):
    nseq = ny * nz
    chans = signal.shape[1]
    half = out_proj.shape[1] // 2
    quarter, middle = chans // 4, chans // 2
    hop = ny // 2
    first, twist, second, back, last = make_tables(nseq)
    rows = twist.shape[1]
    hbm = pl.BlockSpec(memory_space=pltpu.HBM)
    vmem = pl.BlockSpec(memory_space=pltpu.VMEM)
    smem = pl.BlockSpec(memory_space=pltpu.SMEM)
    out = jax.ShapeDtypeStruct((LANES, chans), BF16)
    wide = (nseq, 2 * GROUP, LANES)
    narrow = (nseq, GROUP, LANES)
    tile = (LANES, chans)
    results = pl.pallas_call(
        functools.partial(kernel, ny, nz, nx),
        out_shape=jax.ShapeDtypeStruct((4, LANES, chans), BF16),
        in_specs=[smem] + [hbm] * 10,
        out_specs=vmem,
        scratch_shapes=[
            pltpu.VMEM(tile, BF16),
            pltpu.VMEM(tile, BF16),
            pltpu.VMEM(tile, BF16),
            pltpu.VMEM(first.shape, BF16),
            pltpu.VMEM(twist.shape, F32),
            pltpu.VMEM(second.shape, BF16),
            pltpu.VMEM(back.shape, BF16),
            pltpu.VMEM(last.shape, BF16),
            pltpu.SemaphoreType.DMA((11,)),
            pltpu.VMEM(wide, BF16),
            pltpu.VMEM(wide, BF16),
            pltpu.VMEM(narrow, BF16),
            pltpu.VMEM(narrow, BF16),
            pltpu.VMEM(narrow, BF16),
            pltpu.VMEM(narrow, BF16),
            pltpu.VMEM(wide, BF16),
            pltpu.VMEM(wide, BF16),
            pltpu.VMEM((nseq * 2 * GROUP, LANES), F32),
            pltpu.VMEM((2, GROUP * rows, 2 * LANES), F32),
            pltpu.VMEM((nseq * half, chans), BF16),
            pltpu.VMEM((chans, chans), BF16),
            pltpu.VMEM(tile, BF16),
            pltpu.VMEM(tile, BF16),
            pltpu.VMEM((2, LANES, nx * CORES * quarter), BF16),
            pltpu.VMEM((2, LANES, nx * middle), BF16),
            pltpu.VMEM((2,) + tile, BF16),
            pltpu.VMEM((2,) + tile, BF16),
            pltpu.VMEM((3,) + tile, BF16),
            pltpu.VMEM((nx, 2 * LANES, quarter), F32),
            pltpu.VMEM((nx, 2 * LANES, middle), F32),
            pltpu.VMEM((nx, 2 * LANES, quarter), BF16),
            pltpu.VMEM((nx, 2 * LANES, quarter), BF16),
            pltpu.VMEM((nx, 2 * LANES, middle), BF16),
            pltpu.VMEM((nx, 2 * LANES, middle), BF16),
            pltpu.VMEM((nx - 1, 2 * LANES, quarter), BF16),
            pltpu.VMEM((nx - 1, 2 * LANES, quarter), BF16),
            pltpu.VMEM((nx - 1, 2 * LANES, middle), BF16),
            pltpu.VMEM((nx - 1, 2 * LANES, middle), BF16),
            pltpu.VMEM((LANES, quarter), BF16),
            pltpu.VMEM((LANES, quarter), BF16),
            pltpu.VMEM((LANES, middle), BF16),
            pltpu.VMEM((LANES, middle), BF16),
            pltpu.VMEM(tile, BF16),
            pltpu.VMEM(tile, F32),
            pltpu.SemaphoreType.DMA((4,)),
            pltpu.SemaphoreType.DMA((4,)),
            pltpu.SemaphoreType.DMA,
            pltpu.SemaphoreType.DMA((2, hop)),
            pltpu.SemaphoreType.DMA((2, 2, ny // 2, hop)),
            pltpu.SemaphoreType.DMA((2 * nx,)),
            pltpu.SemaphoreType.DMA((2 * nx,)),
            pltpu.SemaphoreType.DMA((2 * nx,)),
            pltpu.SemaphoreType.DMA((2 * nx,)),
            pltpu.SemaphoreType.DMA((8,)),
            pltpu.SemaphoreType.DMA((8,)),
            pltpu.SemaphoreType.DMA((nx,)),
            pltpu.SemaphoreType.DMA((nx,)),
            pltpu.SemaphoreType.DMA((nx,)),
            pltpu.SemaphoreType.DMA((nx,)),
            pltpu.SemaphoreType.REGULAR,
        ],
        compiler_params=pltpu.CompilerParams(
            collective_id=0, has_side_effects=True, vmem_limit_bytes=VMEM_LIMIT
        ),
    )(
        skip_gain,
        signal,
        gates,
        filters,
        out_proj.T,
        cotangent,
        first,
        twist,
        second,
        back,
        last,
    )
    return tuple(results[n] for n in range(4))


def solution(mesh):
    side = math.isqrt(mesh.shape["seq"])
    nx = mesh.shape["chan"] // CORES
    in_specs = (
        P("seq", "chan"),
        P("seq", "chan"),
        P("seq", "chan"),
        P("chan"),
        P("chan", "seq"),
        P("seq", "chan"),
    )
    out_specs = (P("seq", "chan"),) * 4
    return jax.shard_map(
        functools.partial(local, side, side, nx),
        mesh=mesh,
        in_specs=in_specs,
        out_specs=out_specs,
        check_vma=False,
    )
```
